128 devices in a mesh: dp: 64 (over x, z_hi, y, core), tensor: 2 (over z_lo).
Axes of the slice: x: 4, y: 4, z: 4 (z_hi: 2, z_lo: 2; z = z_hi * 2 + z_lo), core: 2. Of those that a mesh axis runs over, the one named last changes fastest.
Arguments:
- tokens: bfloat16 [16384, 1024], P('dp'), may hold values from -6 to 6
- cotangent: bfloat16 [16384, 1024], P('dp'), may hold values from -16 to 16
- norm_gains: float32 [2, 1024], replicated, may hold values from 0.5 to 1.5
- gains_mean: float32 [2, 1024], replicated, may hold values from -80 to 80
- gains_var: float32 [2, 1024], replicated, may hold values from 819.2 to 3276.8
- kernel: float32 [3, 1024], P(None, 'tensor'), may hold values from -2.5 to 2.5
- kernel_mean: float32 [3, 1024], P(None, 'tensor'), may hold values from -80 to 80
- kernel_var: float32 [3, 1024], P(None, 'tensor'), may hold values from 819.2 to 3276.8
- input_projection: float32 [1024, 3, 1024], P('dp', None, 'tensor'), may hold values from -0.1875 to 0.1875
- input_momentum: float32 [1024, 3, 1024], P('dp', None, 'tensor'), may hold values from -384 to 384
- output_projection: float32 [1024, 1024], P('tensor', 'dp'), may hold values from -0.1875 to 0.1875
- output_momentum: float32 [1024, 1024], P('tensor', 'dp'), may hold values from -384 to 384
- gate_projection: float32 [1024, 4608], P('dp', 'tensor'), may hold values from -0.1875 to 0.1875
- gate_momentum: float32 [1024, 4608], P('dp', 'tensor'), may hold values from -384 to 384
- up_projection: float32 [1024, 4608], P('dp', 'tensor'), may hold values from -0.1875 to 0.1875
- up_momentum: float32 [1024, 4608], P('dp', 'tensor'), may hold values from -384 to 384
- down_projection: float32 [4608, 1024], P('tensor', 'dp'), may hold values from -0.1875 to 0.1875
- down_momentum: float32 [4608, 1024], P('tensor', 'dp'), may hold values from -384 to 384
Outputs:
- mixed: bfloat16 [16384, 1024], P('dp')
- input_grad: float32 [16384, 1024], P('dp')
- in_grad: float32 [1024, 3, 1024], P('dp', None, 'tensor')
- out_grad: float32 [1024, 1024], P('tensor', 'dp')
- gate_grad: float32 [1024, 4608], P('dp', 'tensor')
- up_grad: float32 [1024, 4608], P('dp', 'tensor')
- down_grad: float32 [4608, 1024], P('tensor', 'dp')
- in_momentum_new: float32 [1024, 3, 1024], P('dp', None, 'tensor')
- out_momentum_new: float32 [1024, 1024], P('tensor', 'dp')
- gate_momentum_new: float32 [1024, 4608], P('dp', 'tensor')
- up_momentum_new: float32 [1024, 4608], P('dp', 'tensor')
- down_momentum_new: float32 [4608, 1024], P('tensor', 'dp')
- in_proj_new: float32 [1024, 3, 1024], P('dp', None, 'tensor')
- out_proj_new: float32 [1024, 1024], P('tensor', 'dp')
- gate_proj_new: float32 [1024, 4608], P('dp', 'tensor')
- up_proj_new: float32 [1024, 4608], P('dp', 'tensor')
- down_proj_new: float32 [4608, 1024], P('tensor', 'dp')
- gains_grad: float32 [2, 1024], replicated
- gains_var_new: float32 [2, 1024], replicated
- gains_new: float32 [2, 1024], replicated
- kernel_grad: float32 [3, 1024], P(None, 'tensor')
- kernel_var_new: float32 [3, 1024], P(None, 'tensor')
- kernel_new: float32 [3, 1024], P(None, 'tensor')
The draws below stay inside these ranges and needn't reach their ends.
All inputs are finite; a program needn't handle non-finite values.
Results may differ from the reference program's by a relative error of at most 0.007.
The reference program's roundings to bfloat16 on the way count: a program that leaves them out, or rounds other values in their place, can miss the bound.
Values may be sent and summed in bfloat16 or wider, within the bound.
No kernel may reach another device: no remote copies, remote signals or barrier semaphores. Data moves between devices by JAX's collectives and lax.ppermute only.
A program may use at most 128 MiB of HBM per device.

```python
import math
import jax
import jax.numpy as jnp
from jax import lax

D = 1024
FF = 4608
KS = 3
TOK_DEV = 256
BLK = 64
NS_ITERS = 5
STEP = 10
TOKENS = 16384
N_DP = 64


def raised(array, stream_key, source, target, shards_of, factor):
    owner, partner = [(jnp.arange(array.shape[dim]) // (array.shape[dim] // shards_of)).reshape([-1 if axis == dim else 1 for axis in range(array.ndim)]) for dim in (source, target)]
    chosen = jax.random.permutation(stream_key, shards_of)[partner]
    strong = (owner == chosen) | (owner == (partner + shards_of // 2) % shards_of)
    return jnp.where(strong, factor * array, array)


def level_of(own_key, dims, pieces, least, top_value):
    factor_of, own = 1.0, jax.random.fold_in(own_key, 6)
    for axis_at, parts in pieces:
        heights = jnp.exp(jax.random.uniform(jax.random.fold_in(own, axis_at), (parts,), jnp.float32, least / len(pieces), top_value / len(pieces)))
        factor_of = factor_of * jnp.repeat(heights, dims[axis_at] // parts).reshape([-1 if axis == axis_at else 1 for axis in range(len(dims))])
    return factor_of


def noise(rng, shape, width, bound, cuts=(), dtype=jnp.bfloat16):
    drawn = jax.random.normal(rng, shape, jnp.float32) * width
    if len(cuts) > 0:
        drawn = level_of(rng, shape, cuts, -0.22, 0.18) * drawn
    return jnp.clip(drawn, min=-bound, max=bound).astype(dtype)


def heavy_noise(own_key, extent, width, most, split, heavy, dtype=jnp.bfloat16):
    drawn = width * jax.random.normal(own_key, extent, jnp.float32)
    if split:
        drawn = drawn * level_of(own_key, extent, split, -0.22, 0.18)
    return jnp.clip(raised(drawn, jax.random.fold_in(own_key, 3), *heavy), -most, most).astype(dtype)


def setup_inputs(seed: int = 0) -> dict:
    keys = jax.random.split(jax.random.key(seed), 19)
    return {
        "tokens": noise(keys[0], (TOKENS, D), 1.0, 6.0, ((0, 64),)),
        "cotangent": heavy_noise(keys[1], (TOKENS, D), 1.0, 16.0, ((0, 64),), (0, 1, 64, 4.0)),
        "norm_gains": jnp.clip(1.0 + 0.1 * jax.random.normal(keys[2], (2, D), jnp.float32), 0.5, 1.5),
        "gains_mean": noise(keys[3], (2, D), (0.1 * TOKENS ** 0.5), 80.0, (), jnp.float32),
        "gains_var": jnp.clip(jnp.exp(jax.random.uniform(keys[4], (2, D), jnp.float32, math.log(819.2), math.log(3276.8))), 819.2, 3276.8),
        "kernel": noise(keys[5], (KS, D), 0.6, 2.5, ((1, 2),), jnp.float32),
        "kernel_mean": noise(keys[6], (KS, D), (0.1 * TOKENS ** 0.5), 80.0, ((1, 2),), jnp.float32),
        "kernel_var": jnp.clip(jnp.exp(math.log(3276.8) - 1.3862944 * jax.random.uniform(keys[7], (KS, D), jnp.float32) ** level_of(keys[7], (KS, D), ((1, 2),), -0.2, 0.2)), 819.2, 3276.8),
        "input_projection": noise(keys[8], (D, 3, D), D ** -0.5, 0.1875, ((0, 64), (2, 2)), jnp.float32),
        "input_momentum": noise(keys[9], (D, 3, D), (0.5 * TOKENS ** 0.5), 384.0, ((0, 64), (2, 2)), jnp.float32),
        "output_projection": noise(keys[10], (D, D), D ** -0.5, 0.1875, ((0, 2), (1, 64)), jnp.float32),
        "output_momentum": noise(keys[11], (D, D), (0.5 * TOKENS ** 0.5), 384.0, ((0, 2), (1, 64)), jnp.float32),
        "gate_projection": noise(keys[12], (D, FF), D ** -0.5, 0.1875, ((0, 64), (1, 2)), jnp.float32),
        "gate_momentum": noise(keys[13], (D, FF), (0.5 * TOKENS ** 0.5), 384.0, ((0, 64), (1, 2)), jnp.float32),
        "up_projection": noise(keys[14], (D, FF), D ** -0.5, 0.1875, ((0, 64), (1, 2)), jnp.float32),
        "up_momentum": noise(keys[15], (D, FF), (0.5 * TOKENS ** 0.5), 384.0, ((0, 64), (1, 2)), jnp.float32),
        "down_projection": noise(keys[16], (FF, D), (FF // 4) ** -0.5, 0.1875, ((0, 2), (1, 64)), jnp.float32),
        "down_momentum": noise(keys[17], (FF, D), (0.5 * TOKENS ** 0.5), 384.0, ((0, 2), (1, 64)), jnp.float32),
    }


@jax.custom_vjp
def lowered_weight(v):
    return lax.optimization_barrier(v.astype(jnp.bfloat16)).astype(jnp.float32)

@jax.custom_vjp
def lowered_backward(v):
    return v

def low_keep(v):
    return (lowered_weight(v), None)

def low_pass(kept, grad):
    return (grad,)

def back_keep(v):
    return (v, None)

def back_low(kept, grad):
    return (lowered_weight(grad),)
lowered_weight.defvjp(low_keep, low_pass)
lowered_backward.defvjp(back_keep, back_low)
norm_eps = 1e-05
ortho_eps = 1e-07
coef_a = 3.4445
coef_b = -4.775
coef_c = 2.0315
momentum_decay = 0.95
beta_one = 0.9
beta_two = 0.95
adam_rate = 0.1
adam_eps = 1e-08
highest_precision = lax.Precision.HIGHEST

def rms_norm(values, gain):
    factor = lax.rsqrt(lax.optimization_barrier(jnp.mean(values * values, axis=-1, keepdims=True)) + norm_eps)
    return values * factor * gain

def block_forward(params, hidden_in):
    norm_gains, kernel, input_projection, output_projection, gate_projection, up_projection, down_projection = params
    length = hidden_in.shape[1]
    first_normed = lowered_weight(rms_norm(hidden_in, norm_gains[0]))
    projected_input = lowered_backward(jnp.einsum('phv,vqz->phqz', first_normed, lowered_weight(input_projection), precision=highest_precision))
    b_part = projected_input[:, :, 0]
    c_part = projected_input[:, :, 1]
    x_part = projected_input[:, :, 2]
    product = b_part * x_part
    padded = jnp.pad(product, ((0, 0), (KS - 1, 0), (0, 0)))
    conv_out = jnp.zeros_like(product)
    for offset in range(KS):
        conv_out = conv_out + kernel[offset] * padded[:, offset:offset + length]
    gated_product = lowered_weight(c_part * conv_out)
    branch_path = lowered_backward(jnp.einsum('ahv,vr->ahr', gated_product, lowered_weight(output_projection), precision=highest_precision))
    middle = hidden_in + branch_path
    second_normed = lowered_weight(rms_norm(middle, norm_gains[1]))
    gate_activation = lowered_backward(jnp.einsum('kzt,tc->kzc', second_normed, lowered_weight(gate_projection), precision=highest_precision))
    up_activation = lowered_backward(jnp.einsum('kzt,tc->kzc', second_normed, lowered_weight(up_projection), precision=highest_precision))
    hidden_state = lowered_weight(jax.nn.silu(gate_activation) * up_activation)
    feedforward_output = lowered_backward(jnp.einsum('hjn,nb->hjb', hidden_state, lowered_weight(down_projection), precision=highest_precision))
    return middle + feedforward_output

def orthogonalize(blocks):
    total = lax.optimization_barrier(jnp.sum(blocks * blocks, axis=(0, 2)))
    current = blocks * lax.rsqrt(total + ortho_eps)[None, :, None]
    for sweep in range(NS_ITERS):
        gram = jnp.einsum('rbi,rbj->bij', current, current, precision=highest_precision)
        square = jnp.einsum('bij,bjk->bik', gram, gram, precision=highest_precision)
        current = coef_a * current + jnp.einsum('rbi,bij->rbj', current, coef_b * gram + coef_c * square, precision=highest_precision)
    return current

def muon_update(weight, momentum, grad, transposed):
    momentum_new = momentum_decay * momentum + grad
    oriented = momentum_new.T if transposed else momentum_new
    shape = oriented.shape
    ortho = orthogonalize(oriented.reshape(shape[0], -1, BLK)).reshape(shape)
    if transposed:
        ortho = ortho.T
    muon_rate = 0.25 * math.sqrt(D / BLK)
    return (momentum_new, weight - muon_rate * ortho)

def adam_update(param, mean, var, grad):
    mean_new = beta_one * mean + (1.0 - beta_one) * grad
    var_new = beta_two * var + (1.0 - beta_two) * grad * grad
    mean_hat = mean_new / (1.0 - beta_one ** STEP)
    var_hat = var_new / (1.0 - beta_two ** STEP)
    return (var_new, param - adam_rate * mean_hat / (jnp.sqrt(var_hat) + adam_eps))

def reference(tokens, cotangent, norm_gains, gains_mean, gains_var, kernel, kernel_mean, kernel_var, input_projection, input_momentum, output_projection, output_momentum, gate_projection, gate_momentum, up_projection, up_momentum, down_projection, down_momentum):
    per_group = math.gcd(N_DP, max(1, 4096 // TOK_DEV))
    groups = N_DP // per_group
    tokens_all = tokens.astype(jnp.float32).reshape(groups, per_group, TOK_DEV, D)
    cot_all = cotangent.astype(jnp.float32).reshape(groups, per_group, TOK_DEV, D)
    params = (norm_gains, kernel, input_projection, output_projection, gate_projection, up_projection, down_projection)

    def one_group(totals, batch_pair):
        outputs, pullback = jax.vjp(block_forward, params, batch_pair[0])
        param_grads, input_grad = pullback(batch_pair[1])
        return (jax.tree.map(jnp.add, totals, param_grads), (outputs, input_grad))
    totals, (mixed, input_grad) = lax.scan(one_group, jax.tree.map(jnp.zeros_like, params), (tokens_all, cot_all))
    gains_grad, kernel_grad, in_grad, out_grad, gate_grad, up_grad, down_grad = totals
    in_momentum_new, in_proj_new = muon_update(input_projection, input_momentum, in_grad, False)
    out_momentum_new, out_proj_new = muon_update(output_projection, output_momentum, out_grad, True)
    gate_momentum_new, gate_proj_new = muon_update(gate_projection, gate_momentum, gate_grad, False)
    up_momentum_new, up_proj_new = muon_update(up_projection, up_momentum, up_grad, False)
    down_momentum_new, down_proj_new = muon_update(down_projection, down_momentum, down_grad, True)
    gains_var_new, gains_new = adam_update(norm_gains, gains_mean, gains_var, gains_grad)
    kernel_var_new, kernel_new = adam_update(kernel, kernel_mean, kernel_var, kernel_grad)
    mixed = mixed.reshape(TOKENS, D).astype(jnp.bfloat16)
    input_grad = input_grad.reshape(TOKENS, D)
    return (mixed, input_grad, in_grad, out_grad, gate_grad, up_grad, down_grad, in_momentum_new, out_momentum_new, gate_momentum_new, up_momentum_new, down_momentum_new, in_proj_new, out_proj_new, gate_proj_new, up_proj_new, down_proj_new, gains_grad, gains_var_new, gains_new, kernel_grad, kernel_var_new, kernel_new)
```

```python
import jax
import jax.numpy as jnp
from jax import lax
from jax.sharding import Mesh
from jax.sharding import PartitionSpec as P

D = 1024
FF = 4608
KS = 3
BLK = 64
NS_ITERS = 5
STEP = 10
CHAN = D // 4
HID = FF // 4
HALF = CHAN // 2
ROWS = 32

norm_eps = 1e-05
ortho_eps = 1e-07
coef_a = 3.4445
coef_b = -4.775
coef_c = 2.0315
momentum_decay = 0.95
beta_one = 0.9
beta_two = 0.95
adam_rate = 0.1
adam_eps = 1e-08
highest = lax.Precision.HIGHEST

AXES = ("x", "zh", "y", "c", "zl")
ZAX = ("zh", "zl")
bf16 = jnp.bfloat16
f32 = jnp.float32


def dot_plain(left, right):
    return jnp.dot(left, right, preferred_element_type=f32)


def dot_transposed(left, right):
    return lax.dot_general(left, right, (((1,), (1,)), ((), ())), preferred_element_type=f32)


def norm_forward(values, gain):
    factor = lax.rsqrt(jnp.mean(values * values, axis=-1, keepdims=True) + norm_eps)
    return (factor, values * factor * gain)


def norm_backward(values, factor, gain, grad_normed):
    weighted = grad_normed * gain
    inner = jnp.mean(weighted * values, axis=-1, keepdims=True)
    grad_values = factor * weighted - values * factor * factor * factor * inner
    gain_term = jnp.sum(grad_normed * values * factor, axis=0)
    return (grad_values, gain_term)


def adam_update(param, mean, var, grad):
    mean_new = beta_one * mean + (1.0 - beta_one) * grad
    var_new = beta_two * var + (1.0 - beta_two) * grad * grad
    mean_hat = mean_new / (1.0 - beta_one**STEP)
    var_hat = var_new / (1.0 - beta_two**STEP)
    return (var_new, param - adam_rate * mean_hat / (jnp.sqrt(var_hat) + adam_eps))


def position(axis):
    if axis == "z":
        return lax.axis_index("zh") * 2 + lax.axis_index("zl")
    return lax.axis_index(axis)


def from_ahead(value, axis, step):
    name = ZAX if axis == "z" else axis
    return lax.ppermute(value, name, [((i + step) % 4, i) for i in range(4)])


def swap_cores(value):
    return lax.ppermute(value, "c", [(0, 1), (1, 0)])


def relative(axis, step):
    return lax.rem(position(axis) + step, 4)


def tie(*values):
    return lax.optimization_barrier(values)


def gather_three(values, axes):
    far = [from_ahead(value, axis, 2) for value, axis in zip(values, axes)]
    values, far = tie(values, far)
    near = [[(k, from_ahead(v, axis, k)) for k in (1, 3)] for v, axis in zip(values, axes)]
    return [[(0, v), (2, f), *n] for v, f, n in zip(values, far, near)]


def stack_pieces(pieces, axis):
    shape = pieces[0][1].shape
    buffer = jnp.zeros((4,) + shape, pieces[0][1].dtype)
    zeros = [0] * len(shape)
    for step, piece in pieces:
        buffer = lax.dynamic_update_slice(buffer, piece[None], [relative(axis, step)] + zeros)
    return buffer


def doubled(value, axis):
    name = ZAX if axis == "z" else axis
    where = position(axis)
    got = lax.ppermute(value, name, [(i, i ^ 1) for i in range(4)])
    odd = where % 2 == 1
    pair = jnp.stack([jnp.where(odd, got, value), jnp.where(odd, value, got)])
    other = lax.ppermute(pair, name, [(i, i ^ 2) for i in range(4)])
    high = where >= 2
    return jnp.concatenate([jnp.where(high, other, pair), jnp.where(high, pair, other)])


def give(value, axis, step):
    return from_ahead(value, axis, 4 - step)


def scatter_three(piece_ofs, axes, dtype, staged=True):
    far = [give(p(2).astype(dtype), axis, 2) for p, axis in zip(piece_ofs, axes)]
    sent = [[p(k).astype(dtype) for k in (1, 3)] for p in piece_ofs]
    if staged:
        sent, far = tie(sent, far)
    near = [[give(v, axis, k) for v, k in zip(vs, (1, 3))] for vs, axis in zip(sent, axes)]
    return [p(0) + f + n[0] + n[1] for p, f, n in zip(piece_ofs, far, near)]


def pick(stacked, axis, step):
    return lax.dynamic_index_in_dim(stacked, relative(axis, step), 0, keepdims=False)


def quarters(in_part, out_part, gate_part, up_part, down_part):
    out_t, down_t = out_part.T, down_part.T
    result = []
    for q in range(2):
        chan = slice(q * CHAN, (q + 1) * CHAN)
        hid = slice(q * HID, (q + 1) * HID)
        out_q = out_t[:, chan]
        result.append(
            (
                jnp.concatenate([gate_part[:, hid], in_part[:, 0, chan], out_q[:, :HALF]], axis=1),
                jnp.concatenate([up_part[:, hid], in_part[:, 1, chan], out_q[:, HALF:]], axis=1),
                jnp.concatenate([down_t[:, hid], in_part[:, 2, chan]], axis=1),
            )
        )
    return result


def unpack(first, second):
    pieces = [[], [], [], [], []]
    for packed in (first, second):
        a, b, c = packed[:, :1536], packed[:, 1536:3072], packed[:, 3072:]
        pieces[0].append(jnp.stack([v[:, HID : HID + CHAN] for v in (a, b, c)], axis=1))
        pieces[1].append(a[:, HID + CHAN :])
        pieces[1].append(b[:, HID + CHAN :])
        pieces[2].append(a[:, :HID])
        pieces[3].append(b[:, :HID])
        pieces[4].append(c[:, :HID])
    joined = [jnp.concatenate(p, axis=-1) for p in pieces]
    return joined[0], joined[1].T, joined[2], joined[3], joined[4].T


def to_chip(mine_first, q0, q1):
    keep = jnp.where(mine_first, q0, q1)
    got = swap_cores(jnp.where(mine_first, q1, q0))
    return jnp.where(mine_first, jnp.concatenate([keep, got]), jnp.concatenate([got, keep]))


def to_device(mine_first, chip):
    upper, lower = chip[:16], chip[16:]
    keep = jnp.where(mine_first, upper, lower)
    got = swap_cores(jnp.where(mine_first, lower, upper))
    return jnp.where(mine_first, keep, got), jnp.where(mine_first, got, keep)


def join_halves(value, z_dim):
    shape = value.shape
    split = value.reshape(shape[:z_dim] + (2, 2) + shape[z_dim + 1 :])
    return jnp.concatenate(
        [lax.index_in_dim(split, t, z_dim + 1, keepdims=False) for t in range(2)], axis=-1
    )


def columns_two(value, z_dim):
    early = jnp.concatenate(
        [
            join_halves(value[..., HID : HID + CHAN], z_dim),
            join_halves(value[..., HID + CHAN :], z_dim),
        ],
        axis=-1,
    )
    return early, join_halves(value[..., :HID], z_dim)


def newton_schulz(blocks):
    block_view = blocks.transpose(1, 0, 2)
    gram = jnp.einsum("bri,brj->bij", block_view, block_view, precision=highest)
    total = jnp.trace(gram, axis1=1, axis2=2) + ortho_eps
    gram = gram / total[:, None, None]
    eye = jnp.eye(BLK, dtype=f32)
    factor = None
    for sweep in range(NS_ITERS):
        square = jnp.matmul(gram, gram, precision=highest)
        poly = coef_a * eye + coef_b * gram + coef_c * square
        factor = poly if factor is None else jnp.matmul(factor, poly, precision=highest)
        if sweep < NS_ITERS - 1:
            gram = jnp.matmul(
                jnp.matmul(poly, gram, precision=highest), poly, precision=highest
            )
    factor = factor * lax.rsqrt(total)[:, None, None]
    ortho = jnp.einsum("bri,bij->brj", block_view, factor, precision=highest)
    return ortho.transpose(1, 0, 2)


def per_device(
    tokens,
    cotangent,
    norm_gains,
    gains_mean,
    gains_var,
    kernel,
    kernel_mean,
    kernel_var,
    input_projection,
    input_momentum,
    output_projection,
    output_momentum,
    gate_projection,
    gate_momentum,
    up_projection,
    up_momentum,
    down_projection,
    down_momentum,
):
    token_count = tokens.shape[0]
    core = lax.axis_index("c")
    z_low = lax.axis_index("zl")
    first_core = core == 0
    own_sequence = core == z_low

    parts = quarters(
        input_projection.astype(bf16),
        output_projection.astype(bf16),
        gate_projection.astype(bf16),
        up_projection.astype(bf16),
        down_projection.astype(bf16),
    )
    thirds = to_chip(first_core, *[jnp.concatenate(parts[q], axis=1) for q in range(2)])
    tokens_chip = jnp.where(own_sequence, tokens, swap_cores(tokens))
    cotangent_chip = jnp.where(own_sequence, cotangent, swap_cores(cotangent))
    kernel_other = lax.ppermute(kernel, "zl", [(0, 1), (1, 0)])
    kernel_halves = [jnp.where(z_low == t, kernel, kernel_other) for t in range(2)]
    taps = jnp.concatenate(
        [lax.dynamic_slice(v, (0, core * CHAN), (KS, CHAN)) for v in kernel_halves], axis=1
    )

    thirds, tokens_chip, cotangent_chip, taps = tie(thirds, tokens_chip, cotangent_chip, taps)
    one_a = doubled(thirds[:, :1536], "z")
    one_b = doubled(thirds[:, 1536:3072], "x")
    one_c = doubled(thirds[:, 3072:], "y")
    one_a, one_b, one_c = tie(one_a, one_b, one_c)
    two_a, two_b, two_c = gather_three((one_a, one_b, one_c), "yzx")
    two_a = stack_pieces(two_a, "y")
    two_b = stack_pieces(two_b, "z")
    two_c = stack_pieces(two_c, "x")
    early_a, late_a = columns_two(two_a, 1)
    early_b, late_b = columns_two(two_b.transpose(1, 0, 2, 3), 1)
    early_a, late_a = [v.transpose(1, 0, 2, 3).reshape(256, -1) for v in (early_a, late_a)]
    early_b, late_b = [v.reshape(8, ROWS, -1) for v in (early_b, late_b)]
    early_c, late_c = two_c[..., HID:], two_c[..., :HID]

    def full_a(pieces):
        return stack_pieces(pieces, "x").reshape(D, -1)

    def full_b(pieces):
        return stack_pieces(pieces, "y").transpose(1, 0, 2, 3).reshape(D, -1)

    def full_c(pieces):
        stacked = stack_pieces(pieces, "z")
        split = stacked.reshape((2, 2) + stacked.shape[1:]).transpose(1, 2, 0, 3, 4, 5)
        return jnp.concatenate([split[t].reshape(D, -1) for t in range(2)], axis=1)

    early_a, early_b, early_c = tie(early_a, early_b, early_c)
    early, late, momenta = tie(
        gather_three((early_a, early_b, early_c), "xyz"),
        (late_a, late_b, late_c),
        (input_momentum, output_momentum, gate_momentum, up_momentum, down_momentum),
    )
    early_a, early_b, early_c = early
    late_a, late_b, late_c = gather_three(late, "xyz")
    momentum_parts = quarters(*momenta)
    momentum_chip = to_chip(
        first_core, *[jnp.concatenate(momentum_parts[q], axis=1) for q in range(2)]
    )
    all_a, all_b, low_x = full_a(early_a), full_b(early_b), full_c(early_c)
    low_b, low_c = all_a[:, : 2 * CHAN], all_b[:, : 2 * CHAN]
    out_a, out_b = all_a[:, 2 * CHAN :], all_b[:, 2 * CHAN :]
    low_out = jnp.concatenate(
        [out_a[:, :HALF], out_b[:, :HALF], out_a[:, HALF:], out_b[:, HALF:]], axis=1
    )

    hidden_in = tokens_chip.astype(f32)
    scale_one, normed_full = norm_forward(hidden_in, norm_gains[0])
    first_normed = normed_full.astype(bf16)
    b_part = dot_plain(first_normed, low_b)
    c_part = dot_plain(first_normed, low_c)
    x_part = dot_plain(first_normed, low_x)
    product = b_part * x_part
    padded = jnp.pad(product, ((KS - 1, 0), (0, 0)))
    conv_out = jnp.zeros_like(product)
    for offset in range(KS):
        conv_out = conv_out + taps[offset] * padded[offset : offset + token_count]
    gated_product = (c_part * conv_out).astype(bf16)

    def core_sum(value):
        return value + swap_cores(value)

    middle = hidden_in + core_sum(dot_transposed(gated_product, low_out))
    scale_two, normed_full_two = norm_forward(middle, norm_gains[1])
    second_normed = normed_full_two.astype(bf16)
    second_normed, middle, momentum_chip = tie(second_normed, middle, momentum_chip)
    low_gate, low_up, low_down = full_a(late_a), full_b(late_b), full_c(late_c)
    gate_activation = dot_plain(second_normed, low_gate)
    up_activation = dot_plain(second_normed, low_up)
    sigmoid_gate = jax.nn.sigmoid(gate_activation)
    activated = gate_activation * sigmoid_gate
    hidden_state = (activated * up_activation).astype(bf16)
    mixed_chip = (middle + core_sum(dot_transposed(hidden_state, low_down))).astype(bf16)

    def rows_of(value):
        return value.T.reshape(4, 2, 4, ROWS, token_count)

    def terms_a(act_rows, grad):
        def piece(step):
            rows = lax.dynamic_index_in_dim(act_rows, relative("x", step), 0, keepdims=False)
            return dot_plain(rows.reshape(256, token_count), grad)

        return piece

    def terms_b(act_rows, grad):
        def piece(step):
            rows = lax.dynamic_index_in_dim(act_rows, relative("y", step), 2, keepdims=False)
            return dot_plain(rows.reshape(256, token_count), grad)

        return piece

    def terms_c(act_rows, grad):
        width = grad.shape[1] // 2

        def piece(step):
            target = relative("z", step)
            rows = lax.dynamic_index_in_dim(act_rows, target // 2, 1, keepdims=False)
            half = jnp.where(target % 2 == 0, grad[:, :width], grad[:, width:])
            return dot_plain(rows.reshape(512, token_count), half)

        return piece

    def sends(terms, axis, steps):
        return [give(terms(k).astype(bf16), axis, k) for k in steps]

    down_terms = terms_c(rows_of(cotangent_chip), hidden_state)
    down_far = sends(down_terms, "z", (2,))
    grad_hidden = dot_plain(cotangent_chip, low_down)
    slope = sigmoid_gate * (1.0 + gate_activation * (1.0 - sigmoid_gate))
    grad_gate = (grad_hidden * up_activation * slope).astype(bf16)
    grad_up = (grad_hidden * activated).astype(bf16)
    second_rows = rows_of(second_normed)
    gate_terms = terms_a(second_rows, grad_gate)
    up_terms = terms_b(second_rows, grad_up)
    gate_far = sends(gate_terms, "x", (2,))
    up_far = sends(up_terms, "y", (2,))
    grad_normed_two = core_sum(
        dot_transposed(grad_gate, low_gate) + dot_transposed(grad_up, low_up)
    )
    norm_back_two, gain_two = norm_backward(middle, scale_two, norm_gains[1], grad_normed_two)
    grad_middle = cotangent_chip.astype(f32) + norm_back_two
    grad_branch = grad_middle.astype(bf16)
    far, near, grad_branch = tie(
        (down_far[0], gate_far[0], up_far[0]),
        [[t(k).astype(bf16) for k in (1, 3)] for t in (down_terms, gate_terms, up_terms)],
        grad_branch,
    )
    near = [[give(v, axis, k) for v, k in zip(vs, (1, 3))] for vs, axis in zip(near, "zxy")]
    down_own, gate_own, up_own = [
        t(0) + f + n[0] + n[1] for t, f, n in zip((down_terms, gate_terms, up_terms), far, near)
    ]
    grad_gated = dot_plain(grad_branch, low_out)
    grad_conv = grad_gated * c_part
    grad_c = (grad_gated * conv_out).astype(bf16)
    padded_back = jnp.pad(grad_conv, ((0, KS - 1), (0, 0)))
    kernel_rows = []
    grad_bx = jnp.zeros_like(grad_conv)
    for offset in range(KS):
        kernel_rows.append(jnp.sum(grad_conv * padded[offset : offset + token_count], axis=0))
        begin = KS - 1 - offset
        grad_bx = grad_bx + taps[offset] * padded_back[begin : begin + token_count]
    kernel_local = jnp.stack(kernel_rows)
    grad_b = (grad_bx * x_part).astype(bf16)
    grad_x = (grad_bx * b_part).astype(bf16)
    branch_rows = rows_of(grad_branch)
    first_rows = rows_of(first_normed)
    out_first = jnp.concatenate(
        [gated_product[:, :HALF], gated_product[:, CHAN : CHAN + HALF]], axis=1
    )
    out_second = jnp.concatenate(
        [gated_product[:, HALF:CHAN], gated_product[:, CHAN + HALF :]], axis=1
    )

    def both(in_terms, out_terms):
        return lambda step: jnp.concatenate([in_terms(step), out_terms(step)], axis=1)

    grad_normed_one = core_sum(
        dot_transposed(grad_b, low_b)
        + dot_transposed(grad_c, low_c)
        + dot_transposed(grad_x, low_x)
    )
    norm_back_one, gain_one = norm_backward(hidden_in, scale_one, norm_gains[0], grad_normed_one)
    input_grad_chip = grad_middle + norm_back_one
    small = jnp.concatenate([gain_one, gain_two, kernel_local.reshape(-1)])
    small = small + lax.ppermute(small, "zl", [(0, 1), (1, 0)])
    far_values = (grad_b, grad_c, grad_x, out_first, out_second, branch_rows, first_rows)
    own = (down_own, gate_own, up_own)
    far_values, own, small, input_grad_chip = tie(far_values, own, small, input_grad_chip)
    grad_b, grad_c, grad_x, out_first, out_second, branch_rows, first_rows = far_values
    down_own, gate_own, up_own = own
    small_a, small_b, small_c = scatter_three(
        (
            both(terms_a(first_rows, grad_b), terms_a(branch_rows, out_first)),
            both(terms_b(first_rows, grad_c), terms_b(branch_rows, out_second)),
            terms_c(first_rows, grad_x),
        ),
        "xyz",
        bf16,
    )

    def z_columns(value):
        ends = [0, HID, 2 * HID, 2 * HID + CHAN, 2 * HID + 2 * CHAN]
        ends += [2 * HID + 2 * CHAN + HALF, 2 * HID + 2 * CHAN + 2 * HALF]
        halves = []
        for t in range(2):
            halves.append(
                jnp.concatenate(
                    [value[..., ends[i + t] : ends[i + t + 1]] for i in (0, 2, 4)], axis=-1
                )
            )
        stacked = jnp.stack(halves, axis=1)
        return stacked.reshape((4,) + stacked.shape[2:])

    def stacked_terms(*values):
        return [lambda step, v=v, a=a: pick(v, a, step) for v, a in values]

    sum_a = jnp.concatenate([gate_own, small_a], axis=1).reshape(2, 4, ROWS, -1)
    sum_b = jnp.concatenate([up_own, small_b], axis=1).reshape(4, 2, ROWS, -1)
    sum_c = jnp.concatenate([down_own, small_c], axis=1).reshape(4, 4, ROWS, -1)
    sum_a = sum_a.transpose(1, 0, 2, 3)
    sum_b = z_columns(sum_b.transpose(1, 0, 2, 3))
    sum_a, sum_b, sum_c = tie(sum_a, sum_b, sum_c)
    sum_a, sum_b, sum_c = scatter_three(
        stacked_terms((sum_a, "y"), (sum_b, "z"), (sum_c, "x")), "yzx", bf16
    )
    sum_a, sum_b, sum_c = tie(z_columns(sum_a), sum_b, sum_c)
    sum_a, sum_b, sum_c = scatter_three(
        stacked_terms((sum_a, "z"), (sum_b, "x"), (sum_c, "y")), "zxy", bf16, staged=False
    )
    grad_chip = jnp.concatenate([sum_a, sum_b, sum_c], axis=1)
    grad_chip, mixed_chip, input_grad_chip = tie(grad_chip, mixed_chip, input_grad_chip)

    def to_owner(value):
        got = lax.ppermute(value, ("c", "zl"), [(0, 1), (3, 2)])
        return jnp.where(own_sequence, value, got)

    mixed = to_owner(mixed_chip)
    input_grad = to_owner(input_grad_chip)

    updated = momentum_decay * momentum_chip + grad_chip
    total_columns = updated.shape[1]
    members = 32
    blocks = -(-total_columns // (members * BLK))
    share = blocks * BLK
    filled = jnp.pad(updated, ((0, 0), (0, share * members - total_columns)))
    slices = jnp.pad(small.reshape(members, -1), ((0, 0), (0, 2 * BLK - small.shape[0] // members)))
    slices = slices.reshape(members, 2, BLK).transpose(1, 0, 2)
    slices = jnp.pad(slices, ((0, ROWS - 2), (0, 0), (0, 0)))
    filled = jnp.concatenate([filled.reshape(ROWS, members, share), slices], axis=2)
    plane = ("x", "zh", "y")
    owned = lax.all_to_all(
        filled.reshape(ROWS, -1), plane, split_axis=1, concat_axis=0, tiled=True
    )
    slice_sum = jnp.sum(owned.reshape(members, ROWS, -1)[:, :2, share:], axis=0)
    finished = newton_schulz(owned[:, :share].reshape(D, blocks, BLK)).reshape(D, share)
    terms = []
    for _ in range(3):
        term = lax.reduce_precision(slice_sum, 8, 7)
        terms.append(term)
        slice_sum = slice_sum - term
    terms = jnp.pad(jnp.concatenate(terms, axis=0), ((0, ROWS - 6), (0, 0)))
    terms = jnp.broadcast_to(terms[None], (members, ROWS, BLK)).reshape(D, BLK)
    finished = jnp.concatenate([finished, terms], axis=1).astype(bf16)
    returned = lax.all_to_all(finished, plane, split_axis=0, concat_axis=1, tiled=True)
    returned = returned.reshape(ROWS, members, share + BLK)
    ortho_chip = returned[:, :, :share].reshape(ROWS, -1)[:, :total_columns]
    terms = returned[:6, :, share:].astype(f32)
    summed = (terms[0:2] + terms[2:4] + terms[4:6]).transpose(1, 0, 2).reshape(members, -1)
    summed = summed[:, : small.shape[0] // members].reshape(-1)
    gains_grad = summed[: 2 * D].reshape(2, D)
    tap_sums = summed[2 * D :].reshape(KS, 2, CHAN)
    tap_mine = lax.dynamic_index_in_dim(tap_sums, z_low, 1, keepdims=False)
    tap_other = swap_cores(tap_mine)
    kernel_grad = jnp.where(
        first_core,
        jnp.concatenate([tap_mine, tap_other], axis=1),
        jnp.concatenate([tap_other, tap_mine], axis=1),
    )

    grads = unpack(*to_device(first_core, grad_chip))
    ortho = unpack(*to_device(first_core, ortho_chip))
    momenta = (input_momentum, output_momentum, gate_momentum, up_momentum, down_momentum)
    params = (
        input_projection,
        output_projection,
        gate_projection,
        up_projection,
        down_projection,
    )
    momenta_new = [momentum_decay * m + g for m, g in zip(momenta, grads)]
    muon_rate = 0.25 * (D / BLK) ** 0.5
    params_new = [p - muon_rate * o.astype(f32) for p, o in zip(params, ortho)]
    gains_var_new, gains_new = adam_update(norm_gains, gains_mean, gains_var, gains_grad)
    kernel_var_new, kernel_new = adam_update(kernel, kernel_mean, kernel_var, kernel_grad)
    return (
        mixed,
        input_grad,
        *grads,
        *momenta_new,
        *params_new,
        gains_grad,
        gains_var_new,
        gains_new,
        kernel_grad,
        kernel_var_new,
        kernel_new,
    )


def solution(mesh):
    torus = Mesh(mesh.devices.reshape(4, 2, 4, 2, 2), AXES)
    dp, tensor = ("x", "zh", "y", "c"), "zl"
    token = P(dp, None)
    in_proj, wide, tall = P(dp, None, tensor), P(dp, tensor), P(tensor, dp)
    taps = P(None, tensor)
    matrices = (in_proj, tall, wide, wide, tall)
    in_specs = (token, token, P(), P(), P(), taps, taps, taps) + tuple(
        spec for spec in matrices for _ in range(2)
    )
    out_specs = (token, token) + matrices * 3 + (P(), P(), P(), taps, taps, taps)
    return jax.shard_map(
        per_device, mesh=torus, in_specs=in_specs, out_specs=out_specs, check_vma=False
    )
```

```python
import jax
import jax.numpy as jnp
from jax import lax
from jax.sharding import Mesh
from jax.sharding import PartitionSpec as P

D = 1024
FF = 4608
KS = 3
BLK = 64
NS_ITERS = 5
STEP = 10
CHAN = D // 4
HID = FF // 4
HALF = CHAN // 2
ROWS = 32

norm_eps = 1e-05
ortho_eps = 1e-07
coef_a = 3.4445
coef_b = -4.775
coef_c = 2.0315
momentum_decay = 0.95
beta_one = 0.9
beta_two = 0.95
adam_rate = 0.1
adam_eps = 1e-08
highest = lax.Precision.HIGHEST

AXES = ("x", "zh", "y", "c", "zl")
ZAX = ("zh", "zl")
bf16 = jnp.bfloat16
f32 = jnp.float32


def dot_plain(left, right):
    return jnp.dot(left, right, preferred_element_type=f32)


def dot_transposed(left, right):
    return lax.dot_general(left, right, (((1,), (1,)), ((), ())), preferred_element_type=f32)


def dot_rows(left, right):
    return lax.dot_general(left, right, (((0,), (0,)), ((), ())), preferred_element_type=f32)


def norm_forward(values, gain):
    factor = lax.rsqrt(jnp.mean(values * values, axis=-1, keepdims=True) + norm_eps)
    return (factor, values * factor * gain)


def norm_backward(values, factor, gain, grad_normed):
    weighted = grad_normed * gain
    inner = jnp.mean(weighted * values, axis=-1, keepdims=True)
    grad_values = factor * weighted - values * factor * factor * factor * inner
    gain_term = jnp.sum(grad_normed * values * factor, axis=0)
    return (grad_values, gain_term)


def adam_update(param, mean, var, grad):
    mean_new = beta_one * mean + (1.0 - beta_one) * grad
    var_new = beta_two * var + (1.0 - beta_two) * grad * grad
    mean_hat = mean_new / (1.0 - beta_one**STEP)
    var_hat = var_new / (1.0 - beta_two**STEP)
    return (var_new, param - adam_rate * mean_hat / (jnp.sqrt(var_hat) + adam_eps))


def position(axis):
    if axis == "z":
        return lax.axis_index("zh") * 2 + lax.axis_index("zl")
    return lax.axis_index(axis)


def from_ahead(value, axis, step):
    name = ZAX if axis == "z" else axis
    return lax.ppermute(value, name, [((i + step) % 4, i) for i in range(4)])


def swap_cores(value):
    return lax.ppermute(value, "c", [(0, 1), (1, 0)])


def relative(axis, step):
    return lax.rem(position(axis) + step, 4)


def tie(*values):
    return lax.optimization_barrier(values)


FIRST = ((2,), (1, 3), (1, 3))
SECOND = ((1, 3), (2,), (2,))


def ask(values, axes, plan):
    return [
        [from_ahead(value, axis, k) for k in steps]
        for value, axis, steps in zip(values, axes, plan)
    ]


def by_step(values, first, second):
    return [
        [(0, v), *zip(ks, n), *zip(kf, f)]
        for v, f, n, kf, ks in zip(values, first, second, FIRST, SECOND)
    ]


def gather_three(values, axes):
    got = ask(values, axes, FIRST)
    values, got = tie(values, got)
    return by_step(values, got, ask(values, axes, SECOND))


def stack_pieces(pieces, axis):
    shape = pieces[0][1].shape
    buffer = jnp.zeros((4,) + shape, pieces[0][1].dtype)
    zeros = [0] * len(shape)
    for step, piece in pieces:
        buffer = lax.dynamic_update_slice(buffer, piece[None], [relative(axis, step)] + zeros)
    return buffer


def doubled(value, axis):
    name = ZAX if axis == "z" else axis
    where = position(axis)
    got = lax.ppermute(value, name, [(i, i ^ 1) for i in range(4)])
    odd = where % 2 == 1
    pair = jnp.stack([jnp.where(odd, got, value), jnp.where(odd, value, got)])
    other = lax.ppermute(pair, name, [(i, i ^ 2) for i in range(4)])
    high = where >= 2
    return jnp.concatenate([jnp.where(high, other, pair), jnp.where(high, pair, other)])


def give(value, axis, step):
    return from_ahead(value, axis, 4 - step)


def send(values, axes, plan):
    return [
        [give(v, axis, k) for v, k in zip(vs, steps)]
        for vs, axis, steps in zip(values, axes, plan)
    ]


def terms_for(piece_ofs, plan, dtype):
    return [[p(k).astype(dtype) for k in steps] for p, steps in zip(piece_ofs, plan)]


def scatter_three(piece_ofs, axes, dtype, staged=True):
    got = send(terms_for(piece_ofs, FIRST, dtype), axes, FIRST)
    later = terms_for(piece_ofs, SECOND, dtype)
    if staged:
        later, got = tie(later, got)
    rest = send(later, axes, SECOND)
    return [sum(f + n, p(0)) for p, f, n in zip(piece_ofs, got, rest)]


def pick(stacked, axis, step):
    return lax.dynamic_index_in_dim(stacked, relative(axis, step), 0, keepdims=False)


def quarters(in_part, out_part, gate_part, up_part, down_part):
    out_t, down_t = out_part.T, down_part.T
    result = []
    for q in range(2):
        chan = slice(q * CHAN, (q + 1) * CHAN)
        hid = slice(q * HID, (q + 1) * HID)
        out_q = out_t[:, chan]
        result.append(
            (
                jnp.concatenate([gate_part[:, hid], in_part[:, 0, chan], out_q[:, :HALF]], axis=1),
                jnp.concatenate([up_part[:, hid], in_part[:, 1, chan], out_q[:, HALF:]], axis=1),
                jnp.concatenate([down_t[:, hid], in_part[:, 2, chan]], axis=1),
            )
        )
    return result


def unpack(first, second):
    pieces = [[], [], [], [], []]
    for packed in (first, second):
        a, b, c = packed[:, :1536], packed[:, 1536:3072], packed[:, 3072:]
        pieces[0].append(jnp.stack([v[:, HID : HID + CHAN] for v in (a, b, c)], axis=1))
        pieces[1].append(a[:, HID + CHAN :])
        pieces[1].append(b[:, HID + CHAN :])
        pieces[2].append(a[:, :HID])
        pieces[3].append(b[:, :HID])
        pieces[4].append(c[:, :HID])
    joined = [jnp.concatenate(p, axis=-1) for p in pieces]
    return joined[0], joined[1].T, joined[2], joined[3], joined[4].T


def to_chip(mine_first, q0, q1):
    keep = jnp.where(mine_first, q0, q1)
    got = swap_cores(jnp.where(mine_first, q1, q0))
    return jnp.where(mine_first, jnp.concatenate([keep, got]), jnp.concatenate([got, keep]))


def to_device(mine_first, chip):
    upper, lower = chip[:16], chip[16:]
    keep = jnp.where(mine_first, upper, lower)
    got = swap_cores(jnp.where(mine_first, lower, upper))
    return jnp.where(mine_first, keep, got), jnp.where(mine_first, got, keep)


def join_halves(value, z_dim):
    shape = value.shape
    split = value.reshape(shape[:z_dim] + (2, 2) + shape[z_dim + 1 :])
    return jnp.concatenate(
        [lax.index_in_dim(split, t, z_dim + 1, keepdims=False) for t in range(2)], axis=-1
    )


def columns_two(value, z_dim):
    early = jnp.concatenate(
        [
            join_halves(value[..., HID : HID + CHAN], z_dim),
            join_halves(value[..., HID + CHAN :], z_dim),
        ],
        axis=-1,
    )
    return early, join_halves(value[..., :HID], z_dim)


def newton_schulz(blocks):
    block_view = blocks.transpose(1, 0, 2)
    gram = jnp.einsum("bri,brj->bij", block_view, block_view, precision=highest)
    total = jnp.trace(gram, axis1=1, axis2=2) + ortho_eps
    gram = gram / total[:, None, None]
    eye = jnp.eye(BLK, dtype=f32)
    factor = None
    for sweep in range(NS_ITERS):
        square = jnp.matmul(gram, gram, precision=highest)
        poly = coef_a * eye + coef_b * gram + coef_c * square
        factor = poly if factor is None else jnp.matmul(factor, poly, precision=highest)
        if sweep < NS_ITERS - 1:
            gram = jnp.matmul(
                jnp.matmul(poly, gram, precision=highest), poly, precision=highest
            )
    factor = factor * lax.rsqrt(total)[:, None, None]
    ortho = jnp.einsum("bri,bij->brj", block_view, factor, precision=highest)
    return ortho.transpose(1, 0, 2)


def per_device(
    tokens,
    cotangent,
    norm_gains,
    gains_mean,
    gains_var,
    kernel,
    kernel_mean,
    kernel_var,
    input_projection,
    input_momentum,
    output_projection,
    output_momentum,
    gate_projection,
    gate_momentum,
    up_projection,
    up_momentum,
    down_projection,
    down_momentum,
):
    token_count = tokens.shape[0]
    core = lax.axis_index("c")
    z_low = lax.axis_index("zl")
    first_core = core == 0
    own_sequence = core == z_low

    parts = quarters(
        input_projection.astype(bf16),
        output_projection.astype(bf16),
        gate_projection.astype(bf16),
        up_projection.astype(bf16),
        down_projection.astype(bf16),
    )
    thirds = to_chip(first_core, *[jnp.concatenate(parts[q], axis=1) for q in range(2)])
    tokens_chip = jnp.where(own_sequence, tokens, swap_cores(tokens))
    cotangent_chip = jnp.where(own_sequence, cotangent, swap_cores(cotangent))
    kernel_other = lax.ppermute(kernel, "zl", [(0, 1), (1, 0)])
    kernel_halves = [jnp.where(z_low == t, kernel, kernel_other) for t in range(2)]
    taps = jnp.concatenate(
        [lax.dynamic_slice(v, (0, core * CHAN), (KS, CHAN)) for v in kernel_halves], axis=1
    )

    thirds, tokens_chip, cotangent_chip, taps = tie(thirds, tokens_chip, cotangent_chip, taps)
    one_a = doubled(thirds[:, :1536], "z")
    one_b = doubled(thirds[:, 1536:3072], "x")
    one_c = doubled(thirds[:, 3072:], "y")
    one_a, one_b, one_c = tie(one_a, one_b, one_c)
    two_a, two_b, two_c = gather_three((one_a, one_b, one_c), "yzx")
    two_a = stack_pieces(two_a, "y")
    two_b = stack_pieces(two_b, "z")
    two_c = stack_pieces(two_c, "x")
    early_a, late_a = columns_two(two_a, 1)
    early_b, late_b = columns_two(two_b.transpose(1, 0, 2, 3), 1)
    early_a, late_a = [v.transpose(1, 0, 2, 3).reshape(256, -1) for v in (early_a, late_a)]
    early_b, late_b = [v.reshape(8, ROWS, -1) for v in (early_b, late_b)]
    early_c, late_c = two_c[..., HID:], two_c[..., :HID]

    def full_a(pieces):
        return stack_pieces(pieces, "x").reshape(D, -1)

    def full_b(pieces):
        return stack_pieces(pieces, "y").transpose(1, 0, 2, 3).reshape(D, -1)

    def full_c(pieces):
        stacked = stack_pieces(pieces, "z")
        split = stacked.reshape((2, 2) + stacked.shape[1:]).transpose(1, 2, 0, 3, 4, 5)
        return jnp.concatenate([split[t].reshape(D, -1) for t in range(2)], axis=1)

    early, late = (early_a, early_b, early_c), (late_a, late_b, late_c)
    early, late = tie(early, late)
    widths = [v.shape[-1] for v in early]
    joined = [jnp.concatenate([e, l], axis=-1) for e, l in zip(early, late)]
    early_first = ask(early, "xyz", FIRST)
    momenta = (input_momentum, output_momentum, gate_momentum, up_momentum, down_momentum)
    joined, early_first, momenta = tie(joined, early_first, momenta)
    joined_second = ask(joined, "xyz", SECOND)
    momentum_parts = quarters(*momenta)
    momentum_chip = to_chip(
        first_core, *[jnp.concatenate(momentum_parts[q], axis=1) for q in range(2)]
    )
    late, joined_second, momentum_chip = tie(late, joined_second, momentum_chip)
    late_first = ask(late, "xyz", FIRST)
    early_second = [[v[..., :w] for v in n] for n, w in zip(joined_second, widths)]
    early_a, early_b, early_c = by_step(early, early_first, early_second)
    all_a, all_b, low_x = full_a(early_a), full_b(early_b), full_c(early_c)
    low_b, low_c = all_a[:, : 2 * CHAN], all_b[:, : 2 * CHAN]
    out_a, out_b = all_a[:, 2 * CHAN :], all_b[:, 2 * CHAN :]
    low_out = jnp.concatenate(
        [out_a[:, :HALF], out_b[:, :HALF], out_a[:, HALF:], out_b[:, HALF:]], axis=1
    )

    hidden_in = tokens_chip.astype(f32)
    scale_one, normed_full = norm_forward(hidden_in, norm_gains[0])
    first_normed = normed_full.astype(bf16)
    b_part = dot_plain(first_normed, low_b)
    c_part = dot_plain(first_normed, low_c)
    x_part = dot_plain(first_normed, low_x)
    product = b_part * x_part
    padded = jnp.pad(product, ((KS - 1, 0), (0, 0)))
    conv_out = jnp.zeros_like(product)
    for offset in range(KS):
        conv_out = conv_out + taps[offset] * padded[offset : offset + token_count]
    gated_product = (c_part * conv_out).astype(bf16)
    gated_product, late_first = tie(gated_product, late_first)
    late_second = [[v[..., w:] for v in n] for n, w in zip(joined_second, widths)]
    late_a, late_b, late_c = [dict(v) for v in by_step(late, late_first, late_second)]

    def core_sum(value):
        return value + swap_cores(value)

    middle = hidden_in + core_sum(dot_transposed(gated_product, low_out))
    scale_two, normed_full_two = norm_forward(middle, norm_gains[1])
    second_normed = normed_full_two.astype(bf16)
    gate_pieces = {k: v.reshape(256, -1) for k, v in late_a.items()}
    up_pieces = {k: v.reshape(256, -1) for k, v in late_b.items()}
    down_pieces = {k: v.reshape(512, -1) for k, v in late_c.items()}
    order = (0, 1, 2, 3)

    def rows_of(value):
        return value.T.reshape(4, 2, 4, ROWS, token_count)

    def rows_a(act_rows, step):
        return pick(act_rows, "x", step).reshape(256, token_count)

    def rows_b(act_rows, step):
        rows = lax.dynamic_index_in_dim(act_rows, relative("y", step), 2, keepdims=False)
        return rows.reshape(256, token_count)

    def rows_c(act_rows, step):
        rows = lax.dynamic_index_in_dim(act_rows, relative("z", step) // 2, 1, keepdims=False)
        return rows.reshape(512, token_count)

    def half_c(value, step):
        width = value.shape[1] // 2
        return jnp.where(relative("z", step) % 2 == 0, value[:, :width], value[:, width:])

    second_rows = rows_of(second_normed)
    gate_activation = sum(dot_rows(rows_a(second_rows, k), gate_pieces[k]) for k in order)
    up_activation = sum(dot_rows(rows_b(second_rows, k), up_pieces[k]) for k in order)
    sigmoid_gate = jax.nn.sigmoid(gate_activation)
    activated = gate_activation * sigmoid_gate
    hidden_state = (activated * up_activation).astype(bf16)
    z_even, low_z = z_low == 0, lax.axis_index("zh") == 0

    def terms_a(act_rows, grad):
        return lambda step: dot_plain(rows_a(act_rows, step), grad)

    def terms_b(act_rows, grad):
        return lambda step: dot_plain(rows_b(act_rows, step), grad)

    def terms_c(act_rows, grad):
        return lambda step: dot_plain(rows_c(act_rows, step), half_c(grad, step))

    cot_rows = rows_of(cotangent_chip)
    down_terms = terms_c(cot_rows, hidden_state)
    down_first = send(terms_for([down_terms], ((1, 3),), bf16), "z", ((1, 3),))
    hidden_back = {k: dot_rows(rows_c(cot_rows, k), down_pieces[k]) for k in order}
    back_same, back_other = hidden_back[0] + hidden_back[2], hidden_back[1] + hidden_back[3]
    grad_hidden = jnp.concatenate(
        [jnp.where(z_even, back_same, back_other), jnp.where(z_even, back_other, back_same)], axis=1
    )
    slope = sigmoid_gate * (1.0 + gate_activation * (1.0 - sigmoid_gate))
    grad_gate = (grad_hidden * up_activation * slope).astype(bf16)
    grad_up = (grad_hidden * activated).astype(bf16)
    gate_terms = terms_a(second_rows, grad_gate)
    up_terms = terms_b(second_rows, grad_up)
    wide_terms = (gate_terms, up_terms, down_terms)
    first = send(terms_for(wide_terms[:2], FIRST, bf16), "xy", FIRST) + down_first
    back_gate = stack_pieces([(k, dot_transposed(gate_pieces[k], grad_gate)) for k in order], "x")
    back_up = stack_pieces([(k, dot_transposed(up_pieces[k], grad_up)) for k in order], "y")
    back_up = back_up.reshape(4, 8, ROWS, token_count).transpose(1, 0, 2, 3)
    back_rows = back_gate.reshape(D, token_count) + back_up.reshape(D, token_count)
    first, back_rows = tie(first, back_rows)
    grad_normed_two = core_sum(back_rows.T)
    norm_back_two, gain_two = norm_backward(middle, scale_two, norm_gains[1], grad_normed_two)
    grad_middle = cotangent_chip.astype(f32) + norm_back_two
    grad_branch = grad_middle.astype(bf16)
    first, later = tie(first, terms_for(wide_terms, SECOND, bf16))
    second = send(later, "xyz", SECOND)
    grad_gated = dot_plain(grad_branch, low_out)
    grad_conv = grad_gated * c_part
    grad_c = (grad_gated * conv_out).astype(bf16)
    padded_back = jnp.pad(grad_conv, ((0, KS - 1), (0, 0)))
    kernel_rows = []
    grad_bx = jnp.zeros_like(grad_conv)
    for offset in range(KS):
        kernel_rows.append(jnp.sum(grad_conv * padded[offset : offset + token_count], axis=0))
        begin = KS - 1 - offset
        grad_bx = grad_bx + taps[offset] * padded_back[begin : begin + token_count]
    kernel_local = jnp.stack(kernel_rows)
    grad_b = (grad_bx * x_part).astype(bf16)
    grad_x = (grad_bx * b_part).astype(bf16)
    branch_rows = rows_of(grad_branch)
    first_rows = rows_of(first_normed)
    out_first = jnp.concatenate(
        [gated_product[:, :HALF], gated_product[:, CHAN : CHAN + HALF]], axis=1
    )
    out_second = jnp.concatenate(
        [gated_product[:, HALF:CHAN], gated_product[:, CHAN + HALF :]], axis=1
    )

    def both(in_terms, out_terms):
        return lambda step: jnp.concatenate([in_terms(step), out_terms(step)], axis=1)

    grad_normed_one = core_sum(
        dot_transposed(grad_b, low_b)
        + dot_transposed(grad_c, low_c)
        + dot_transposed(grad_x, low_x)
    )
    norm_back_one, gain_one = norm_backward(hidden_in, scale_one, norm_gains[0], grad_normed_one)
    input_grad_chip = grad_middle + norm_back_one
    small = jnp.concatenate([gain_one, gain_two, kernel_local.reshape(-1)])
    small = small + lax.ppermute(small, "zl", [(0, 1), (1, 0)])
    far_values = (grad_b, grad_c, grad_x, out_first, out_second, branch_rows, first_rows)
    far_values, second = tie(far_values, second)
    grad_b, grad_c, grad_x, out_first, out_second, branch_rows, first_rows = far_values
    gate_own, up_own, down_own = [
        sum(f + n, t(0)) for t, f, n in zip(wide_terms, first, second)
    ]
    small_a, small_b, small_c = scatter_three(
        (
            both(terms_a(first_rows, grad_b), terms_a(branch_rows, out_first)),
            both(terms_b(first_rows, grad_c), terms_b(branch_rows, out_second)),
            terms_c(first_rows, grad_x),
        ),
        "xyz",
        bf16,
    )

    def z_columns(value):
        ends = [0, HID, 2 * HID, 2 * HID + CHAN, 2 * HID + 2 * CHAN]
        ends += [2 * HID + 2 * CHAN + HALF, 2 * HID + 2 * CHAN + 2 * HALF]
        halves = []
        for t in range(2):
            halves.append(
                jnp.concatenate(
                    [value[..., ends[i + t] : ends[i + t + 1]] for i in (0, 2, 4)], axis=-1
                )
            )
        stacked = jnp.stack(halves, axis=1)
        return stacked.reshape((4,) + stacked.shape[2:])

    def stacked_terms(*values):
        return [lambda step, v=v, a=a: pick(v, a, step) for v, a in values]

    sum_a = jnp.concatenate([gate_own, small_a], axis=1).reshape(2, 4, ROWS, -1)
    sum_b = jnp.concatenate([up_own, small_b], axis=1).reshape(4, 2, ROWS, -1)
    sum_c = jnp.concatenate([down_own, small_c], axis=1).reshape(4, 4, ROWS, -1)
    sum_a = sum_a.transpose(1, 0, 2, 3)
    sum_b = z_columns(sum_b.transpose(1, 0, 2, 3))
    sum_a, sum_b, sum_c, small, input_grad_chip = tie(
        sum_a, sum_b, sum_c, small, input_grad_chip
    )
    sum_a, sum_b, sum_c = scatter_three(
        stacked_terms((sum_a, "y"), (sum_b, "z"), (sum_c, "x")), "yzx", bf16
    )
    sum_a, sum_b, sum_c = tie(z_columns(sum_a), sum_b, sum_c)
    sum_a, sum_b, sum_c = scatter_three(
        stacked_terms((sum_a, "z"), (sum_b, "x"), (sum_c, "y")), "zxy", bf16, staged=False
    )
    grad_chip = jnp.concatenate([sum_a, sum_b, sum_c], axis=1)
    grad_chip, hidden_state, input_grad_chip = tie(grad_chip, hidden_state, input_grad_chip)
    down_out = {k: dot_transposed(down_pieces[k], half_c(hidden_state, k)) for k in order}
    out_same = down_out[0] + jnp.where(z_even, down_out[1], down_out[3])
    out_other = down_out[2] + jnp.where(z_even, down_out[3], down_out[1])
    down_rows = jnp.stack(
        [
            jnp.where(low_z, out_same, out_other).reshape(4, 128, token_count),
            jnp.where(low_z, out_other, out_same).reshape(4, 128, token_count),
        ],
        axis=1,
    ).reshape(D, token_count)
    mixed_chip = (middle + core_sum(down_rows.T)).astype(bf16)

    def to_owner(value):
        got = lax.ppermute(value, ("c", "zl"), [(0, 1), (3, 2)])
        return jnp.where(own_sequence, value, got)

    mixed = to_owner(mixed_chip)
    input_grad = to_owner(input_grad_chip)

    updated = momentum_decay * momentum_chip + grad_chip
    total_columns = updated.shape[1]
    members = 32
    blocks = -(-total_columns // (members * BLK))
    share = blocks * BLK
    filled = jnp.pad(updated, ((0, 0), (0, share * members - total_columns)))
    slices = jnp.pad(small.reshape(members, -1), ((0, 0), (0, 2 * BLK - small.shape[0] // members)))
    slices = slices.reshape(members, 2, BLK).transpose(1, 0, 2)
    slices = jnp.pad(slices, ((0, ROWS - 2), (0, 0), (0, 0)))
    filled = jnp.concatenate([filled.reshape(ROWS, members, share), slices], axis=2)
    plane = ("x", "zh", "y")
    owned = lax.all_to_all(
        filled.reshape(ROWS, -1), plane, split_axis=1, concat_axis=0, tiled=True
    )
    slice_sum = jnp.sum(owned.reshape(members, ROWS, -1)[:, :2, share:], axis=0)
    finished = newton_schulz(owned[:, :share].reshape(D, blocks, BLK)).reshape(D, share)
    terms = []
    for _ in range(3):
        term = lax.reduce_precision(slice_sum, 8, 7)
        terms.append(term)
        slice_sum = slice_sum - term
    terms = jnp.pad(jnp.concatenate(terms, axis=0), ((0, ROWS - 6), (0, 0)))
    terms = jnp.broadcast_to(terms[None], (members, ROWS, BLK)).reshape(D, BLK)
    finished = jnp.concatenate([finished, terms], axis=1).astype(bf16)
    returned = lax.all_to_all(finished, plane, split_axis=0, concat_axis=1, tiled=True)
    returned = returned.reshape(ROWS, members, share + BLK)
    ortho_chip = returned[:, :, :share].reshape(ROWS, -1)[:, :total_columns]
    terms = returned[:6, :, share:].astype(f32)
    summed = (terms[0:2] + terms[2:4] + terms[4:6]).transpose(1, 0, 2).reshape(members, -1)
    summed = summed[:, : small.shape[0] // members].reshape(-1)
    gains_grad = summed[: 2 * D].reshape(2, D)
    tap_sums = summed[2 * D :].reshape(KS, 2, CHAN)
    tap_mine = lax.dynamic_index_in_dim(tap_sums, z_low, 1, keepdims=False)
    tap_other = swap_cores(tap_mine)
    kernel_grad = jnp.where(
        first_core,
        jnp.concatenate([tap_mine, tap_other], axis=1),
        jnp.concatenate([tap_other, tap_mine], axis=1),
    )

    grads = unpack(*to_device(first_core, grad_chip))
    ortho = unpack(*to_device(first_core, ortho_chip))
    momenta = (input_momentum, output_momentum, gate_momentum, up_momentum, down_momentum)
    params = (
        input_projection,
        output_projection,
        gate_projection,
        up_projection,
        down_projection,
    )
    momenta_new = [momentum_decay * m + g for m, g in zip(momenta, grads)]
    muon_rate = 0.25 * (D / BLK) ** 0.5
    params_new = [p - muon_rate * o.astype(f32) for p, o in zip(params, ortho)]
    gains_var_new, gains_new = adam_update(norm_gains, gains_mean, gains_var, gains_grad)
    kernel_var_new, kernel_new = adam_update(kernel, kernel_mean, kernel_var, kernel_grad)
    return (
        mixed,
        input_grad,
        *grads,
        *momenta_new,
        *params_new,
        gains_grad,
        gains_var_new,
        gains_new,
        kernel_grad,
        kernel_var_new,
        kernel_new,
    )


def solution(mesh):
    torus = Mesh(mesh.devices.reshape(4, 2, 4, 2, 2), AXES)
    dp, tensor = ("x", "zh", "y", "c"), "zl"
    token = P(dp, None)
    in_proj, wide, tall = P(dp, None, tensor), P(dp, tensor), P(tensor, dp)
    taps = P(None, tensor)
    matrices = (in_proj, tall, wide, wide, tall)
    in_specs = (token, token, P(), P(), P(), taps, taps, taps) + tuple(
        spec for spec in matrices for _ in range(2)
    )
    out_specs = (token, token) + matrices * 3 + (P(), P(), P(), taps, taps, taps)
    return jax.shard_map(
        per_device, mesh=torus, in_specs=in_specs, out_specs=out_specs, check_vma=False
    )
```

```python
import jax
import jax.numpy as jnp
from jax import lax
from jax.sharding import Mesh
from jax.sharding import PartitionSpec as P

D = 1024
FF = 4608
KS = 3
BLK = 64
NS_ITERS = 5
STEP = 10
CHAN = D // 4
HID = FF // 4
HALF = CHAN // 2
ROWS = 32

norm_eps = 1e-05
ortho_eps = 1e-07
coef_a = 3.4445
coef_b = -4.775
coef_c = 2.0315
momentum_decay = 0.95
beta_one = 0.9
beta_two = 0.95
adam_rate = 0.1
adam_eps = 1e-08
highest = lax.Precision.HIGHEST

AXES = ("x", "zh", "y", "c", "zl")
ZAX = ("zh", "zl")
bf16 = jnp.bfloat16
f32 = jnp.float32


def dot_plain(left, right):
    return jnp.dot(left, right, preferred_element_type=f32)


def dot_transposed(left, right):
    return lax.dot_general(left, right, (((1,), (1,)), ((), ())), preferred_element_type=f32)


def dot_rows(left, right):
    return lax.dot_general(left, right, (((0,), (0,)), ((), ())), preferred_element_type=f32)


def norm_forward(values, gain):
    factor = lax.rsqrt(jnp.mean(values * values, axis=-1, keepdims=True) + norm_eps)
    return (factor, values * factor * gain)


def norm_backward(values, factor, gain, grad_normed):
    weighted = grad_normed * gain
    inner = jnp.mean(weighted * values, axis=-1, keepdims=True)
    grad_values = factor * weighted - values * factor * factor * factor * inner
    gain_term = jnp.sum(grad_normed * values * factor, axis=0)
    return (grad_values, gain_term)


def adam_update(param, mean, var, grad):
    mean_new = beta_one * mean + (1.0 - beta_one) * grad
    var_new = beta_two * var + (1.0 - beta_two) * grad * grad
    mean_hat = mean_new / (1.0 - beta_one**STEP)
    var_hat = var_new / (1.0 - beta_two**STEP)
    return (var_new, param - adam_rate * mean_hat / (jnp.sqrt(var_hat) + adam_eps))


def position(axis):
    if axis == "z":
        return lax.axis_index("zh") * 2 + lax.axis_index("zl")
    return lax.axis_index(axis)


def from_ahead(value, axis, step):
    name = ZAX if axis == "z" else axis
    return lax.ppermute(value, name, [((i + step) % 4, i) for i in range(4)])


def swap_cores(value):
    return lax.ppermute(value, "c", [(0, 1), (1, 0)])


def relative(axis, step):
    return lax.rem(position(axis) + step, 4)


def tie(*values):
    return lax.optimization_barrier(values)


FIRST = ((2,), (1, 3), (1, 3))
SECOND = ((1, 3), (2,), (2,))


def ask(values, axes, plan):
    return [
        [from_ahead(value, axis, k) for k in steps]
        for value, axis, steps in zip(values, axes, plan)
    ]


def by_step(values, first, second):
    return [
        [(0, v), *zip(ks, n), *zip(kf, f)]
        for v, f, n, kf, ks in zip(values, first, second, FIRST, SECOND)
    ]


def gather_three(values, axes):
    got = ask(values, axes, FIRST)
    values, got = tie(values, got)
    return by_step(values, got, ask(values, axes, SECOND))


def stack_pieces(pieces, axis):
    shape = pieces[0][1].shape
    buffer = jnp.zeros((4,) + shape, pieces[0][1].dtype)
    zeros = [0] * len(shape)
    for step, piece in pieces:
        buffer = lax.dynamic_update_slice(buffer, piece[None], [relative(axis, step)] + zeros)
    return buffer


def doubled(value, axis):
    name = ZAX if axis == "z" else axis
    where = position(axis)
    got = lax.ppermute(value, name, [(i, i ^ 1) for i in range(4)])
    odd = where % 2 == 1
    pair = jnp.stack([jnp.where(odd, got, value), jnp.where(odd, value, got)])
    other = lax.ppermute(pair, name, [(i, i ^ 2) for i in range(4)])
    high = where >= 2
    return jnp.concatenate([jnp.where(high, other, pair), jnp.where(high, pair, other)])


def give(value, axis, step):
    return from_ahead(value, axis, 4 - step)


def send(values, axes, plan):
    return [
        [give(v, axis, k) for v, k in zip(vs, steps)]
        for vs, axis, steps in zip(values, axes, plan)
    ]


def terms_for(piece_ofs, plan, dtype):
    return [[p(k).astype(dtype) for k in steps] for p, steps in zip(piece_ofs, plan)]


def scatter_three(piece_ofs, axes, dtype, staged=True):
    got = send(terms_for(piece_ofs, FIRST, dtype), axes, FIRST)
    later = terms_for(piece_ofs, SECOND, dtype)
    if staged:
        later, got = tie(later, got)
    rest = send(later, axes, SECOND)
    return [sum(f + n, p(0)) for p, f, n in zip(piece_ofs, got, rest)]


def pick(stacked, axis, step):
    return lax.dynamic_index_in_dim(stacked, relative(axis, step), 0, keepdims=False)


def quarters(in_part, out_part, gate_part, up_part, down_part):
    out_t, down_t = out_part.T, down_part.T
    result = []
    for q in range(2):
        chan = slice(q * CHAN, (q + 1) * CHAN)
        hid = slice(q * HID, (q + 1) * HID)
        out_q = out_t[:, chan]
        result.append(
            (
                jnp.concatenate([gate_part[:, hid], in_part[:, 0, chan], out_q[:, :HALF]], axis=1),
                jnp.concatenate([up_part[:, hid], in_part[:, 1, chan], out_q[:, HALF:]], axis=1),
                jnp.concatenate([down_t[:, hid], in_part[:, 2, chan]], axis=1),
            )
        )
    return result


def unpack(first, second):
    pieces = [[], [], [], [], []]
    for packed in (first, second):
        a, b, c = packed[:, :1536], packed[:, 1536:3072], packed[:, 3072:]
        pieces[0].append(jnp.stack([v[:, HID : HID + CHAN] for v in (a, b, c)], axis=1))
        pieces[1].append(a[:, HID + CHAN :])
        pieces[1].append(b[:, HID + CHAN :])
        pieces[2].append(a[:, :HID])
        pieces[3].append(b[:, :HID])
        pieces[4].append(c[:, :HID])
    joined = [jnp.concatenate(p, axis=-1) for p in pieces]
    return joined[0], joined[1].T, joined[2], joined[3], joined[4].T


def to_chip(mine_first, q0, q1):
    keep = jnp.where(mine_first, q0, q1)
    got = swap_cores(jnp.where(mine_first, q1, q0))
    return jnp.where(mine_first, jnp.concatenate([keep, got]), jnp.concatenate([got, keep]))


def to_device(mine_first, chip):
    upper, lower = chip[:16], chip[16:]
    keep = jnp.where(mine_first, upper, lower)
    got = swap_cores(jnp.where(mine_first, lower, upper))
    return jnp.where(mine_first, keep, got), jnp.where(mine_first, got, keep)


def join_halves(value, z_dim):
    shape = value.shape
    split = value.reshape(shape[:z_dim] + (2, 2) + shape[z_dim + 1 :])
    return jnp.concatenate(
        [lax.index_in_dim(split, t, z_dim + 1, keepdims=False) for t in range(2)], axis=-1
    )


def columns_two(value, z_dim):
    early = jnp.concatenate(
        [
            join_halves(value[..., HID : HID + CHAN], z_dim),
            join_halves(value[..., HID + CHAN :], z_dim),
        ],
        axis=-1,
    )
    return early, join_halves(value[..., :HID], z_dim)


def newton_schulz(columns):
    width = columns.shape[1]
    block_of = jnp.arange(width) // BLK
    same = block_of[:, None] == block_of[None, :]
    total = jnp.sum(columns * columns, axis=0, keepdims=True)
    total = jnp.sum(jnp.where(same, total.T, 0.0), axis=0, keepdims=True) + ortho_eps

    def multiply(left, right):
        return jnp.matmul(left, right, precision=highest)

    gram = lax.dot_general(
        columns, columns, (((0,), (0,)), ((), ())), precision=highest, preferred_element_type=f32
    )
    gram = jnp.where(same, gram / total, 0.0)
    eye = jnp.eye(width, dtype=f32)
    factor = None
    for sweep in range(NS_ITERS):
        poly = coef_a * eye + coef_b * gram + coef_c * multiply(gram, gram)
        factor = poly if factor is None else multiply(factor, poly)
        if sweep < NS_ITERS - 1:
            gram = multiply(multiply(poly, gram), poly)
    return multiply(columns, factor * lax.rsqrt(total))


def per_device(
    tokens,
    cotangent,
    norm_gains,
    gains_mean,
    gains_var,
    kernel,
    kernel_mean,
    kernel_var,
    input_projection,
    input_momentum,
    output_projection,
    output_momentum,
    gate_projection,
    gate_momentum,
    up_projection,
    up_momentum,
    down_projection,
    down_momentum,
):
    token_count = tokens.shape[0]
    core = lax.axis_index("c")
    z_low = lax.axis_index("zl")
    first_core = core == 0
    own_sequence = core == z_low

    parts = quarters(
        input_projection.astype(bf16),
        output_projection.astype(bf16),
        gate_projection.astype(bf16),
        up_projection.astype(bf16),
        down_projection.astype(bf16),
    )
    thirds = to_chip(first_core, *[jnp.concatenate(parts[q], axis=1) for q in range(2)])
    tokens_chip = jnp.where(own_sequence, tokens, swap_cores(tokens))
    cotangent_chip = jnp.where(own_sequence, cotangent, swap_cores(cotangent))
    kernel_other = lax.ppermute(kernel, "zl", [(0, 1), (1, 0)])
    kernel_halves = [jnp.where(z_low == t, kernel, kernel_other) for t in range(2)]
    taps = jnp.concatenate(
        [lax.dynamic_slice(v, (0, core * CHAN), (KS, CHAN)) for v in kernel_halves], axis=1
    )

    one_a = doubled(thirds[:, :1536], "z")
    one_b = doubled(thirds[:, 1536:3072], "x")
    one_c = doubled(thirds[:, 3072:], "y")
    one_a, one_b, one_c, tokens_chip, cotangent_chip, taps = tie(
        one_a, one_b, one_c, tokens_chip, cotangent_chip, taps
    )
    two_a, two_b, two_c = gather_three((one_a, one_b, one_c), "yzx")
    two_a = stack_pieces(two_a, "y")
    two_b = stack_pieces(two_b, "z")
    two_c = stack_pieces(two_c, "x")
    early_a, late_a = columns_two(two_a, 1)
    early_b, late_b = columns_two(two_b.transpose(1, 0, 2, 3), 1)
    early_a, late_a = [v.transpose(1, 0, 2, 3).reshape(256, -1) for v in (early_a, late_a)]
    early_b, late_b = [v.reshape(8, ROWS, -1) for v in (early_b, late_b)]
    early_c, late_c = two_c[..., HID:], two_c[..., :HID]

    def full_a(pieces):
        return stack_pieces(pieces, "x").reshape(D, -1)

    def full_b(pieces):
        return stack_pieces(pieces, "y").transpose(1, 0, 2, 3).reshape(D, -1)

    def full_c(pieces):
        stacked = stack_pieces(pieces, "z")
        split = stacked.reshape((2, 2) + stacked.shape[1:]).transpose(1, 2, 0, 3, 4, 5)
        return jnp.concatenate([split[t].reshape(D, -1) for t in range(2)], axis=1)

    early, late = (early_a, early_b, early_c), (late_a, late_b, late_c)
    early, late = tie(early, late)
    widths = [v.shape[-1] for v in early]
    joined = [jnp.concatenate([e, l], axis=-1) for e, l in zip(early, late)]
    early_first = ask(early, "xyz", FIRST)
    momenta = (input_momentum, output_momentum, gate_momentum, up_momentum, down_momentum)
    joined, early_first, momenta = tie(joined, early_first, momenta)
    joined_second = ask(joined, "xyz", SECOND)
    momentum_parts = quarters(*momenta)
    momentum_chip = to_chip(
        first_core, *[jnp.concatenate(momentum_parts[q], axis=1) for q in range(2)]
    )
    late, joined_second, momentum_chip = tie(late, joined_second, momentum_chip)
    late_first = ask(late, "xyz", FIRST)
    early_second = [[v[..., :w] for v in n] for n, w in zip(joined_second, widths)]
    early_a, early_b, early_c = by_step(early, early_first, early_second)
    all_a, all_b, low_x = full_a(early_a), full_b(early_b), full_c(early_c)
    low_b, low_c = all_a[:, : 2 * CHAN], all_b[:, : 2 * CHAN]
    out_a, out_b = all_a[:, 2 * CHAN :], all_b[:, 2 * CHAN :]
    low_out = jnp.concatenate(
        [out_a[:, :HALF], out_b[:, :HALF], out_a[:, HALF:], out_b[:, HALF:]], axis=1
    )

    hidden_in = tokens_chip.astype(f32)
    scale_one, normed_full = norm_forward(hidden_in, norm_gains[0])
    first_normed = normed_full.astype(bf16)
    b_part = dot_plain(first_normed, low_b)
    c_part = dot_plain(first_normed, low_c)
    x_part = dot_plain(first_normed, low_x)
    product = b_part * x_part
    padded = jnp.pad(product, ((KS - 1, 0), (0, 0)))
    conv_out = jnp.zeros_like(product)
    for offset in range(KS):
        conv_out = conv_out + taps[offset] * padded[offset : offset + token_count]
    gated_product = (c_part * conv_out).astype(bf16)
    gated_product, late_first = tie(gated_product, late_first)
    late_second = [[v[..., w:] for v in n] for n, w in zip(joined_second, widths)]
    late_a, late_b, late_c = [dict(v) for v in by_step(late, late_first, late_second)]

    def core_sum(value):
        return value + swap_cores(value)

    middle = hidden_in + core_sum(dot_transposed(gated_product, low_out))
    scale_two, normed_full_two = norm_forward(middle, norm_gains[1])
    second_normed = normed_full_two.astype(bf16)
    gate_pieces = {k: v.reshape(256, -1) for k, v in late_a.items()}
    up_pieces = {k: v.reshape(256, -1) for k, v in late_b.items()}
    down_pieces = {k: v.reshape(512, -1) for k, v in late_c.items()}
    order = (0, 1, 2, 3)

    def rows_of(value):
        return value.T.reshape(4, 2, 4, ROWS, token_count)

    def rows_a(act_rows, step):
        return pick(act_rows, "x", step).reshape(256, token_count)

    def rows_b(act_rows, step):
        rows = lax.dynamic_index_in_dim(act_rows, relative("y", step), 2, keepdims=False)
        return rows.reshape(256, token_count)

    def rows_c(act_rows, step):
        rows = lax.dynamic_index_in_dim(act_rows, relative("z", step) // 2, 1, keepdims=False)
        return rows.reshape(512, token_count)

    def half_c(value, step):
        width = value.shape[1] // 2
        return jnp.where(relative("z", step) % 2 == 0, value[:, :width], value[:, width:])

    second_rows = rows_of(second_normed)
    gate_activation = sum(dot_rows(rows_a(second_rows, k), gate_pieces[k]) for k in order)
    up_activation = sum(dot_rows(rows_b(second_rows, k), up_pieces[k]) for k in order)
    sigmoid_gate = jax.nn.sigmoid(gate_activation)
    activated = gate_activation * sigmoid_gate
    hidden_state = (activated * up_activation).astype(bf16)
    z_even, low_z = z_low == 0, lax.axis_index("zh") == 0

    def terms_a(act_rows, grad):
        return lambda step: dot_plain(rows_a(act_rows, step), grad)

    def terms_b(act_rows, grad):
        return lambda step: dot_plain(rows_b(act_rows, step), grad)

    def terms_c(act_rows, grad):
        return lambda step: dot_plain(rows_c(act_rows, step), half_c(grad, step))

    cot_rows = rows_of(cotangent_chip)
    down_terms = terms_c(cot_rows, hidden_state)
    down_first = send(terms_for([down_terms], ((1, 3),), bf16), "z", ((1, 3),))
    hidden_back = {k: dot_rows(rows_c(cot_rows, k), down_pieces[k]) for k in order}
    back_same, back_other = hidden_back[0] + hidden_back[2], hidden_back[1] + hidden_back[3]
    grad_hidden = jnp.concatenate(
        [jnp.where(z_even, back_same, back_other), jnp.where(z_even, back_other, back_same)], axis=1
    )
    slope = sigmoid_gate * (1.0 + gate_activation * (1.0 - sigmoid_gate))
    grad_gate = (grad_hidden * up_activation * slope).astype(bf16)
    grad_up = (grad_hidden * activated).astype(bf16)
    gate_terms = terms_a(second_rows, grad_gate)
    up_terms = terms_b(second_rows, grad_up)
    wide_terms = (gate_terms, up_terms, down_terms)
    first = send(terms_for(wide_terms[:2], FIRST, bf16), "xy", FIRST) + down_first
    back_gate = stack_pieces([(k, dot_transposed(gate_pieces[k], grad_gate)) for k in order], "x")
    back_up = stack_pieces([(k, dot_transposed(up_pieces[k], grad_up)) for k in order], "y")
    back_up = back_up.reshape(4, 8, ROWS, token_count).transpose(1, 0, 2, 3)
    back_rows = back_gate.reshape(D, token_count) + back_up.reshape(D, token_count)
    first, back_rows = tie(first, back_rows)
    grad_normed_two = core_sum(back_rows.T)
    norm_back_two, gain_two = norm_backward(middle, scale_two, norm_gains[1], grad_normed_two)
    grad_middle = cotangent_chip.astype(f32) + norm_back_two
    grad_branch = grad_middle.astype(bf16)
    first, later = tie(first, terms_for(wide_terms, SECOND, bf16))
    second = send(later, "xyz", SECOND)
    grad_gated = dot_plain(grad_branch, low_out)
    grad_conv = grad_gated * c_part
    grad_c = (grad_gated * conv_out).astype(bf16)
    padded_back = jnp.pad(grad_conv, ((0, KS - 1), (0, 0)))
    kernel_rows = []
    grad_bx = jnp.zeros_like(grad_conv)
    for offset in range(KS):
        kernel_rows.append(jnp.sum(grad_conv * padded[offset : offset + token_count], axis=0))
        begin = KS - 1 - offset
        grad_bx = grad_bx + taps[offset] * padded_back[begin : begin + token_count]
    kernel_local = jnp.stack(kernel_rows)
    grad_b = (grad_bx * x_part).astype(bf16)
    grad_x = (grad_bx * b_part).astype(bf16)
    branch_rows = rows_of(grad_branch)
    first_rows = rows_of(first_normed)
    out_first = jnp.concatenate(
        [gated_product[:, :HALF], gated_product[:, CHAN : CHAN + HALF]], axis=1
    )
    out_second = jnp.concatenate(
        [gated_product[:, HALF:CHAN], gated_product[:, CHAN + HALF :]], axis=1
    )

    def both(in_terms, out_terms):
        return lambda step: jnp.concatenate([in_terms(step), out_terms(step)], axis=1)

    grad_normed_one = core_sum(
        dot_transposed(grad_b, low_b)
        + dot_transposed(grad_c, low_c)
        + dot_transposed(grad_x, low_x)
    )
    norm_back_one, gain_one = norm_backward(hidden_in, scale_one, norm_gains[0], grad_normed_one)
    input_grad_chip = grad_middle + norm_back_one
    small = jnp.concatenate([gain_one, gain_two, kernel_local.reshape(-1)])
    small = small + lax.ppermute(small, "zl", [(0, 1), (1, 0)])
    far_values = (grad_b, grad_c, grad_x, out_first, out_second, branch_rows, first_rows)
    far_values, second = tie(far_values, second)
    grad_b, grad_c, grad_x, out_first, out_second, branch_rows, first_rows = far_values
    gate_own, up_own, down_own = [
        sum(f + n, t(0)) for t, f, n in zip(wide_terms, first, second)
    ]
    small_a, small_b, small_c = scatter_three(
        (
            both(terms_a(first_rows, grad_b), terms_a(branch_rows, out_first)),
            both(terms_b(first_rows, grad_c), terms_b(branch_rows, out_second)),
            terms_c(first_rows, grad_x),
        ),
        "xyz",
        bf16,
    )

    def z_columns(value):
        ends = [0, HID, 2 * HID, 2 * HID + CHAN, 2 * HID + 2 * CHAN]
        ends += [2 * HID + 2 * CHAN + HALF, 2 * HID + 2 * CHAN + 2 * HALF]
        halves = []
        for t in range(2):
            halves.append(
                jnp.concatenate(
                    [value[..., ends[i + t] : ends[i + t + 1]] for i in (0, 2, 4)], axis=-1
                )
            )
        stacked = jnp.stack(halves, axis=1)
        return stacked.reshape((4,) + stacked.shape[2:])

    def stacked_terms(*values):
        return [lambda step, v=v, a=a: pick(v, a, step) for v, a in values]

    sum_a = jnp.concatenate([gate_own, small_a], axis=1).reshape(2, 4, ROWS, -1)
    sum_b = jnp.concatenate([up_own, small_b], axis=1).reshape(4, 2, ROWS, -1)
    sum_c = jnp.concatenate([down_own, small_c], axis=1).reshape(4, 4, ROWS, -1)
    sum_a = sum_a.transpose(1, 0, 2, 3)
    sum_b = z_columns(sum_b.transpose(1, 0, 2, 3))
    sum_a, sum_b, sum_c, small, input_grad_chip, hidden_state = tie(
        sum_a, sum_b, sum_c, small, input_grad_chip, hidden_state
    )
    down_out = {k: dot_transposed(half_c(hidden_state, k), down_pieces[k]) for k in order}
    out_same = down_out[0] + jnp.where(z_even, down_out[1], down_out[3])
    out_other = down_out[2] + jnp.where(z_even, down_out[3], down_out[1])
    halves = jnp.where(low_z, out_same, out_other), jnp.where(low_z, out_other, out_same)
    down_sum = jnp.concatenate(
        [half[:, 128 * i : 128 * (i + 1)] for i in range(4) for half in halves], axis=1
    )
    mixed_chip = (middle + core_sum(down_sum)).astype(bf16)
    sum_a, sum_b, sum_c = scatter_three(
        stacked_terms((sum_a, "y"), (sum_b, "z"), (sum_c, "x")), "yzx", bf16
    )
    sum_a, sum_b, sum_c, mixed_chip = tie(z_columns(sum_a), sum_b, sum_c, mixed_chip)
    sum_a, sum_b, sum_c = scatter_three(
        stacked_terms((sum_a, "z"), (sum_b, "x"), (sum_c, "y")), "zxy", bf16, staged=False
    )
    grad_chip = jnp.concatenate([sum_a, sum_b, sum_c], axis=1)
    grad_quarters = to_device(first_core, grad_chip)

    grad_quarters, mixed_chip, input_grad_chip = tie(grad_quarters, mixed_chip, input_grad_chip)

    def to_owner(value):
        got = lax.ppermute(value, ("c", "zl"), [(0, 1), (3, 2)])
        return jnp.where(own_sequence, value, got)

    mixed = to_owner(mixed_chip)
    input_grad = to_owner(input_grad_chip)

    updated = momentum_decay * momentum_chip + grad_chip
    total_columns = updated.shape[1]
    members = 32
    blocks = -(-total_columns // (members * BLK))
    share = blocks * BLK
    filled = jnp.pad(updated, ((0, 0), (0, share * members - total_columns)))
    slices = jnp.pad(small.reshape(members, -1), ((0, 0), (0, 2 * BLK - small.shape[0] // members)))
    slices = slices.reshape(members, 2, BLK).transpose(1, 0, 2)
    slices = jnp.pad(slices, ((0, ROWS - 2), (0, 0), (0, 0)))
    filled = jnp.concatenate([filled.reshape(ROWS, members, share), slices], axis=2)
    plane = ("x", "zh", "y")
    owned = lax.all_to_all(
        filled.reshape(ROWS, -1), plane, split_axis=1, concat_axis=0, tiled=True
    )
    slice_sum = jnp.sum(owned.reshape(members, ROWS, -1)[:, :2, share:], axis=0)
    finished = newton_schulz(owned[:, :share])
    terms = []
    for _ in range(3):
        term = lax.reduce_precision(slice_sum, 8, 7)
        terms.append(term)
        slice_sum = slice_sum - term
    terms = jnp.pad(jnp.concatenate(terms, axis=0), ((0, ROWS - 6), (0, 0)))
    terms = jnp.broadcast_to(terms[None], (members, ROWS, BLK)).reshape(D, BLK)
    finished = jnp.concatenate([finished, terms], axis=1).astype(bf16)
    returned = lax.all_to_all(finished, plane, split_axis=0, concat_axis=1, tiled=True)
    returned = returned.reshape(ROWS, members, share + BLK)
    ortho_chip = returned[:, :, :share].reshape(ROWS, -1)[:, :total_columns]
    terms = returned[:6, :, share:].astype(f32)
    summed = (terms[0:2] + terms[2:4] + terms[4:6]).transpose(1, 0, 2).reshape(members, -1)
    summed = summed[:, : small.shape[0] // members].reshape(-1)
    gains_grad = summed[: 2 * D].reshape(2, D)
    tap_sums = summed[2 * D :].reshape(KS, 2, CHAN)
    tap_mine = lax.dynamic_index_in_dim(tap_sums, z_low, 1, keepdims=False)
    tap_other = swap_cores(tap_mine)
    kernel_grad = jnp.where(
        first_core,
        jnp.concatenate([tap_mine, tap_other], axis=1),
        jnp.concatenate([tap_other, tap_mine], axis=1),
    )

    grads = unpack(*grad_quarters)
    ortho = unpack(*to_device(first_core, ortho_chip))
    momenta = (input_momentum, output_momentum, gate_momentum, up_momentum, down_momentum)
    params = (
        input_projection,
        output_projection,
        gate_projection,
        up_projection,
        down_projection,
    )
    momenta_new = [momentum_decay * m + g for m, g in zip(momenta, grads)]
    muon_rate = 0.25 * (D / BLK) ** 0.5
    params_new = [p - muon_rate * o.astype(f32) for p, o in zip(params, ortho)]
    gains_var_new, gains_new = adam_update(norm_gains, gains_mean, gains_var, gains_grad)
    kernel_var_new, kernel_new = adam_update(kernel, kernel_mean, kernel_var, kernel_grad)
    return (
        mixed,
        input_grad,
        *grads,
        *momenta_new,
        *params_new,
        gains_grad,
        gains_var_new,
        gains_new,
        kernel_grad,
        kernel_var_new,
        kernel_new,
    )


def solution(mesh):
    torus = Mesh(mesh.devices.reshape(4, 2, 4, 2, 2), AXES)
    dp, tensor = ("x", "zh", "y", "c"), "zl"
    token = P(dp, None)
    in_proj, wide, tall = P(dp, None, tensor), P(dp, tensor), P(tensor, dp)
    taps = P(None, tensor)
    matrices = (in_proj, tall, wide, wide, tall)
    in_specs = (token, token, P(), P(), P(), taps, taps, taps) + tuple(
        spec for spec in matrices for _ in range(2)
    )
    out_specs = (token, token) + matrices * 3 + (P(), P(), P(), taps, taps, taps)
    return jax.shard_map(
        per_device, mesh=torus, in_specs=in_specs, out_specs=out_specs, check_vma=False
    )
```

```python
import jax
import jax.numpy as jnp
from jax import lax
from jax.sharding import Mesh
from jax.sharding import PartitionSpec as P

D = 1024
FF = 4608
KS = 3
BLK = 64
NS_ITERS = 5
STEP = 10
CHAN = D // 4
HID = FF // 4
HALF = CHAN // 2
ROWS = 32

norm_eps = 1e-05
ortho_eps = 1e-07
coef_a = 3.4445
coef_b = -4.775
coef_c = 2.0315
momentum_decay = 0.95
beta_one = 0.9
beta_two = 0.95
adam_rate = 0.1
adam_eps = 1e-08
highest = lax.Precision.HIGHEST

AXES = ("x", "zh", "y", "c", "zl")
ZAX = ("zh", "zl")
bf16 = jnp.bfloat16
f32 = jnp.float32


def dot_plain(left, right):
    return jnp.dot(left, right, preferred_element_type=f32)


def dot_transposed(left, right):
    return lax.dot_general(left, right, (((1,), (1,)), ((), ())), preferred_element_type=f32)


def dot_rows(left, right):
    return lax.dot_general(left, right, (((0,), (0,)), ((), ())), preferred_element_type=f32)


def norm_forward(values, gain):
    factor = lax.rsqrt(jnp.mean(values * values, axis=-1, keepdims=True) + norm_eps)
    return (factor, values * factor * gain)


def norm_backward(values, factor, gain, grad_normed):
    weighted = grad_normed * gain
    inner = jnp.mean(weighted * values, axis=-1, keepdims=True)
    grad_values = factor * weighted - values * factor * factor * factor * inner
    gain_term = jnp.sum(grad_normed * values * factor, axis=0)
    return (grad_values, gain_term)


def adam_update(param, mean, var, grad):
    mean_new = beta_one * mean + (1.0 - beta_one) * grad
    var_new = beta_two * var + (1.0 - beta_two) * grad * grad
    mean_hat = mean_new / (1.0 - beta_one**STEP)
    var_hat = var_new / (1.0 - beta_two**STEP)
    return (var_new, param - adam_rate * mean_hat / (jnp.sqrt(var_hat) + adam_eps))


def position(axis):
    if axis == "z":
        return lax.axis_index("zh") * 2 + lax.axis_index("zl")
    return lax.axis_index(axis)


def from_ahead(value, axis, step):
    name = ZAX if axis == "z" else axis
    return lax.ppermute(value, name, [((i + step) % 4, i) for i in range(4)])


def swap_cores(value):
    return lax.ppermute(value, "c", [(0, 1), (1, 0)])


def relative(axis, step):
    return lax.rem(position(axis) + step, 4)


def tie(*values):
    return lax.optimization_barrier(values)


FIRST = ((2,), (1, 3), (1, 3))
SECOND = ((1, 3), (2,), (2,))


def ask(values, axes, plan):
    return [
        [from_ahead(value, axis, k) for k in steps]
        for value, axis, steps in zip(values, axes, plan)
    ]


def by_step(values, first, second):
    return [
        [(0, v), *zip(ks, n), *zip(kf, f)]
        for v, f, n, kf, ks in zip(values, first, second, FIRST, SECOND)
    ]


def gather_three(values, axes):
    got = ask(values, axes, FIRST)
    values, got = tie(values, got)
    return by_step(values, got, ask(values, axes, SECOND))


def stack_pieces(pieces, axis):
    shape = pieces[0][1].shape
    buffer = jnp.zeros((4,) + shape, pieces[0][1].dtype)
    zeros = [0] * len(shape)
    for step, piece in pieces:
        buffer = lax.dynamic_update_slice(buffer, piece[None], [relative(axis, step)] + zeros)
    return buffer


def doubled(value, axis):
    name = ZAX if axis == "z" else axis
    where = position(axis)
    got = lax.ppermute(value, name, [(i, i ^ 1) for i in range(4)])
    odd = where % 2 == 1
    pair = jnp.stack([jnp.where(odd, got, value), jnp.where(odd, value, got)])
    other = lax.ppermute(pair, name, [(i, i ^ 2) for i in range(4)])
    high = where >= 2
    return jnp.concatenate([jnp.where(high, other, pair), jnp.where(high, pair, other)])


def give(value, axis, step):
    return from_ahead(value, axis, 4 - step)


def send(values, axes, plan):
    return [
        [give(v, axis, k) for v, k in zip(vs, steps)]
        for vs, axis, steps in zip(values, axes, plan)
    ]


def terms_for(piece_ofs, plan, dtype):
    return [[p(k).astype(dtype) for k in steps] for p, steps in zip(piece_ofs, plan)]


def scatter_three(piece_ofs, axes, dtype, staged=True):
    got = send(terms_for(piece_ofs, FIRST, dtype), axes, FIRST)
    later = terms_for(piece_ofs, SECOND, dtype)
    if staged:
        later, got = tie(later, got)
    rest = send(later, axes, SECOND)
    return [sum(f + n, p(0)) for p, f, n in zip(piece_ofs, got, rest)]


def pick(stacked, axis, step):
    return lax.dynamic_index_in_dim(stacked, relative(axis, step), 0, keepdims=False)


def quarters(in_part, out_part, gate_part, up_part, down_part):
    out_t, down_t = out_part.T, down_part.T
    result = []
    for q in range(2):
        chan = slice(q * CHAN, (q + 1) * CHAN)
        hid = slice(q * HID, (q + 1) * HID)
        out_q = out_t[:, chan]
        result.append(
            (
                jnp.concatenate([gate_part[:, hid], in_part[:, 0, chan], out_q[:, :HALF]], axis=1),
                jnp.concatenate([up_part[:, hid], in_part[:, 1, chan], out_q[:, HALF:]], axis=1),
                jnp.concatenate([down_t[:, hid], in_part[:, 2, chan]], axis=1),
            )
        )
    return result


def unpack(first, second):
    pieces = [[], [], [], [], []]
    for packed in (first, second):
        a, b, c = packed[:, :1536], packed[:, 1536:3072], packed[:, 3072:]
        pieces[0].append(jnp.stack([v[:, HID : HID + CHAN] for v in (a, b, c)], axis=1))
        pieces[1].append(a[:, HID + CHAN :])
        pieces[1].append(b[:, HID + CHAN :])
        pieces[2].append(a[:, :HID])
        pieces[3].append(b[:, :HID])
        pieces[4].append(c[:, :HID])
    joined = [jnp.concatenate(p, axis=-1) for p in pieces]
    return joined[0], joined[1].T, joined[2], joined[3], joined[4].T


def to_chip(mine_first, q0, q1):
    keep = jnp.where(mine_first, q0, q1)
    got = swap_cores(jnp.where(mine_first, q1, q0))
    return jnp.where(mine_first, jnp.concatenate([keep, got]), jnp.concatenate([got, keep]))


def to_device(mine_first, chip):
    upper, lower = chip[:16], chip[16:]
    keep = jnp.where(mine_first, upper, lower)
    got = swap_cores(jnp.where(mine_first, lower, upper))
    return jnp.where(mine_first, keep, got), jnp.where(mine_first, got, keep)


def join_halves(value, z_dim):
    shape = value.shape
    split = value.reshape(shape[:z_dim] + (2, 2) + shape[z_dim + 1 :])
    return jnp.concatenate(
        [lax.index_in_dim(split, t, z_dim + 1, keepdims=False) for t in range(2)], axis=-1
    )


def columns_two(value, z_dim):
    early = jnp.concatenate(
        [
            join_halves(value[..., HID : HID + CHAN], z_dim),
            join_halves(value[..., HID + CHAN :], z_dim),
        ],
        axis=-1,
    )
    return early, join_halves(value[..., :HID], z_dim)


def newton_schulz(columns):
    width = columns.shape[1]
    block_of = jnp.arange(width) // BLK
    same = block_of[:, None] == block_of[None, :]
    total = jnp.sum(columns * columns, axis=0, keepdims=True)
    total = jnp.sum(jnp.where(same, total.T, 0.0), axis=0, keepdims=True) + ortho_eps

    def multiply(left, right):
        return jnp.matmul(left, right, precision=highest)

    gram = lax.dot_general(
        columns, columns, (((0,), (0,)), ((), ())), precision=highest, preferred_element_type=f32
    )
    gram = jnp.where(same, gram / total, 0.0)
    eye = jnp.eye(width, dtype=f32)
    factor = None
    for sweep in range(NS_ITERS):
        poly = coef_a * eye + coef_b * gram + coef_c * multiply(gram, gram)
        factor = poly if factor is None else multiply(factor, poly)
        if sweep < NS_ITERS - 1:
            gram = multiply(multiply(poly, gram), poly)
    return multiply(columns, factor * lax.rsqrt(total))


def per_device(
    tokens,
    cotangent,
    norm_gains,
    gains_mean,
    gains_var,
    kernel,
    kernel_mean,
    kernel_var,
    input_projection,
    input_momentum,
    output_projection,
    output_momentum,
    gate_projection,
    gate_momentum,
    up_projection,
    up_momentum,
    down_projection,
    down_momentum,
):
    token_count = tokens.shape[0]
    core = lax.axis_index("c")
    z_low = lax.axis_index("zl")
    first_core = core == 0
    own_sequence = core == z_low

    parts = quarters(
        input_projection.astype(bf16),
        output_projection.astype(bf16),
        gate_projection.astype(bf16),
        up_projection.astype(bf16),
        down_projection.astype(bf16),
    )
    thirds = to_chip(first_core, *[jnp.concatenate(parts[q], axis=1) for q in range(2)])
    tokens_chip = jnp.where(own_sequence, tokens, swap_cores(tokens))
    cotangent_chip = jnp.where(own_sequence, cotangent, swap_cores(cotangent))
    kernel_other = lax.ppermute(kernel, "zl", [(0, 1), (1, 0)])
    kernel_halves = [jnp.where(z_low == t, kernel, kernel_other) for t in range(2)]
    taps = jnp.concatenate(
        [lax.dynamic_slice(v, (0, core * CHAN), (KS, CHAN)) for v in kernel_halves], axis=1
    )

    thirds, tokens_chip, cotangent_chip, taps = tie(thirds, tokens_chip, cotangent_chip, taps)
    one_a = doubled(thirds[:, :1536], "z")
    one_b = doubled(thirds[:, 1536:3072], "x")
    one_c = doubled(thirds[:, 3072:], "y")
    one_a, one_b, one_c = tie(one_a, one_b, one_c)
    two_a, two_b, two_c = gather_three((one_a, one_b, one_c), "yzx")
    two_a = stack_pieces(two_a, "y")
    two_b = stack_pieces(two_b, "z")
    two_c = stack_pieces(two_c, "x")
    early_a, late_a = columns_two(two_a, 1)
    early_b, late_b = columns_two(two_b.transpose(1, 0, 2, 3), 1)
    early_a, late_a = [v.transpose(1, 0, 2, 3).reshape(256, -1) for v in (early_a, late_a)]
    early_b, late_b = [v.reshape(8, ROWS, -1) for v in (early_b, late_b)]
    early_c, late_c = two_c[..., HID:], two_c[..., :HID]

    def full_a(pieces):
        return stack_pieces(pieces, "x").reshape(D, -1)

    def full_b(pieces):
        return stack_pieces(pieces, "y").transpose(1, 0, 2, 3).reshape(D, -1)

    def full_c(pieces):
        stacked = stack_pieces(pieces, "z")
        split = stacked.reshape((2, 2) + stacked.shape[1:]).transpose(1, 2, 0, 3, 4, 5)
        return jnp.concatenate([split[t].reshape(D, -1) for t in range(2)], axis=1)

    early, late = (early_a, early_b, early_c), (late_a, late_b, late_c)
    early, late = tie(early, late)
    widths = [v.shape[-1] for v in early]
    joined = [jnp.concatenate([e, l], axis=-1) for e, l in zip(early, late)]
    early_first = ask(early, "xyz", FIRST)
    momenta = (input_momentum, output_momentum, gate_momentum, up_momentum, down_momentum)
    joined, early_first, momenta = tie(joined, early_first, momenta)
    joined_second = ask(joined, "xyz", SECOND)
    momentum_parts = quarters(*momenta)
    momentum_chip = to_chip(
        first_core, *[jnp.concatenate(momentum_parts[q], axis=1) for q in range(2)]
    )
    late, joined_second, momentum_chip = tie(late, joined_second, momentum_chip)
    late_first = ask(late, "xyz", FIRST)
    early_second = [[v[..., :w] for v in n] for n, w in zip(joined_second, widths)]
    early_a, early_b, early_c = by_step(early, early_first, early_second)
    all_a, all_b, low_x = full_a(early_a), full_b(early_b), full_c(early_c)
    low_b, low_c = all_a[:, : 2 * CHAN], all_b[:, : 2 * CHAN]
    out_a, out_b = all_a[:, 2 * CHAN :], all_b[:, 2 * CHAN :]
    low_out = jnp.concatenate(
        [out_a[:, :HALF], out_b[:, :HALF], out_a[:, HALF:], out_b[:, HALF:]], axis=1
    )

    hidden_in = tokens_chip.astype(f32)
    scale_one, normed_full = norm_forward(hidden_in, norm_gains[0])
    first_normed = normed_full.astype(bf16)
    b_part = dot_plain(first_normed, low_b)
    c_part = dot_plain(first_normed, low_c)
    x_part = dot_plain(first_normed, low_x)
    product = b_part * x_part
    padded = jnp.pad(product, ((KS - 1, 0), (0, 0)))
    conv_out = jnp.zeros_like(product)
    for offset in range(KS):
        conv_out = conv_out + taps[offset] * padded[offset : offset + token_count]
    gated_product = (c_part * conv_out).astype(bf16)
    gated_product, late_first = tie(gated_product, late_first)
    late_second = [[v[..., w:] for v in n] for n, w in zip(joined_second, widths)]
    late_a, late_b, late_c = [dict(v) for v in by_step(late, late_first, late_second)]

    def core_sum(value):
        return value + swap_cores(value)

    middle = hidden_in + core_sum(dot_transposed(gated_product, low_out))
    scale_two, normed_full_two = norm_forward(middle, norm_gains[1])
    second_normed = normed_full_two.astype(bf16)
    gate_pieces = {k: v.reshape(256, -1) for k, v in late_a.items()}
    up_pieces = {k: v.reshape(256, -1) for k, v in late_b.items()}
    down_pieces = {k: v.reshape(512, -1) for k, v in late_c.items()}
    order = (0, 1, 2, 3)

    def rows_of(value):
        return value.T.reshape(4, 2, 4, ROWS, token_count)

    def rows_a(act_rows, step):
        return pick(act_rows, "x", step).reshape(256, token_count)

    def rows_b(act_rows, step):
        rows = lax.dynamic_index_in_dim(act_rows, relative("y", step), 2, keepdims=False)
        return rows.reshape(256, token_count)

    def rows_c(act_rows, step):
        rows = lax.dynamic_index_in_dim(act_rows, relative("z", step) // 2, 1, keepdims=False)
        return rows.reshape(512, token_count)

    def half_c(value, step):
        width = value.shape[1] // 2
        return jnp.where(relative("z", step) % 2 == 0, value[:, :width], value[:, width:])

    second_rows = rows_of(second_normed)
    gate_activation = sum(dot_rows(rows_a(second_rows, k), gate_pieces[k]) for k in order)
    up_activation = sum(dot_rows(rows_b(second_rows, k), up_pieces[k]) for k in order)
    sigmoid_gate = jax.nn.sigmoid(gate_activation)
    activated = gate_activation * sigmoid_gate
    hidden_state = (activated * up_activation).astype(bf16)
    z_even, low_z = z_low == 0, lax.axis_index("zh") == 0

    def terms_a(act_rows, grad):
        return lambda step: dot_plain(rows_a(act_rows, step), grad)

    def terms_b(act_rows, grad):
        return lambda step: dot_plain(rows_b(act_rows, step), grad)

    def terms_c(act_rows, grad):
        return lambda step: dot_plain(rows_c(act_rows, step), half_c(grad, step))

    cot_rows = rows_of(cotangent_chip)
    down_terms = terms_c(cot_rows, hidden_state)
    down_first = send(terms_for([down_terms], ((1, 3),), bf16), "z", ((1, 3),))
    hidden_back = {k: dot_rows(rows_c(cot_rows, k), down_pieces[k]) for k in order}
    back_same, back_other = hidden_back[0] + hidden_back[2], hidden_back[1] + hidden_back[3]
    grad_hidden = jnp.concatenate(
        [jnp.where(z_even, back_same, back_other), jnp.where(z_even, back_other, back_same)], axis=1
    )
    slope = sigmoid_gate * (1.0 + gate_activation * (1.0 - sigmoid_gate))
    grad_gate = (grad_hidden * up_activation * slope).astype(bf16)
    grad_up = (grad_hidden * activated).astype(bf16)
    gate_terms = terms_a(second_rows, grad_gate)
    up_terms = terms_b(second_rows, grad_up)
    wide_terms = (gate_terms, up_terms, down_terms)
    first = send(terms_for(wide_terms[:2], FIRST, bf16), "xy", FIRST) + down_first
    back_gate = stack_pieces([(k, dot_transposed(gate_pieces[k], grad_gate)) for k in order], "x")
    back_up = stack_pieces([(k, dot_transposed(up_pieces[k], grad_up)) for k in order], "y")
    back_up = back_up.reshape(4, 8, ROWS, token_count).transpose(1, 0, 2, 3)
    back_rows = back_gate.reshape(D, token_count) + back_up.reshape(D, token_count)
    first, back_rows = tie(first, back_rows)
    grad_normed_two = core_sum(back_rows.T)
    norm_back_two, gain_two = norm_backward(middle, scale_two, norm_gains[1], grad_normed_two)
    grad_middle = cotangent_chip.astype(f32) + norm_back_two
    grad_branch = grad_middle.astype(bf16)
    first, later = tie(first, terms_for(wide_terms, SECOND, bf16))
    second = send(later, "xyz", SECOND)
    grad_gated = dot_plain(grad_branch, low_out)
    grad_conv = grad_gated * c_part
    grad_c = (grad_gated * conv_out).astype(bf16)
    padded_back = jnp.pad(grad_conv, ((0, KS - 1), (0, 0)))
    kernel_rows = []
    grad_bx = jnp.zeros_like(grad_conv)
    for offset in range(KS):
        kernel_rows.append(jnp.sum(grad_conv * padded[offset : offset + token_count], axis=0))
        begin = KS - 1 - offset
        grad_bx = grad_bx + taps[offset] * padded_back[begin : begin + token_count]
    kernel_local = jnp.stack(kernel_rows)
    grad_b = (grad_bx * x_part).astype(bf16)
    grad_x = (grad_bx * b_part).astype(bf16)
    branch_rows = rows_of(grad_branch)
    first_rows = rows_of(first_normed)
    out_first = jnp.concatenate(
        [gated_product[:, :HALF], gated_product[:, CHAN : CHAN + HALF]], axis=1
    )
    out_second = jnp.concatenate(
        [gated_product[:, HALF:CHAN], gated_product[:, CHAN + HALF :]], axis=1
    )

    def both(in_terms, out_terms):
        return lambda step: jnp.concatenate([in_terms(step), out_terms(step)], axis=1)

    grad_normed_one = core_sum(
        dot_transposed(grad_b, low_b)
        + dot_transposed(grad_c, low_c)
        + dot_transposed(grad_x, low_x)
    )
    norm_back_one, gain_one = norm_backward(hidden_in, scale_one, norm_gains[0], grad_normed_one)
    input_grad_chip = grad_middle + norm_back_one
    small = jnp.concatenate([gain_one, gain_two, kernel_local.reshape(-1)])
    small = small + lax.ppermute(small, "zl", [(0, 1), (1, 0)])
    far_values = (grad_b, grad_c, grad_x, out_first, out_second, branch_rows, first_rows)
    far_values, second = tie(far_values, second)
    grad_b, grad_c, grad_x, out_first, out_second, branch_rows, first_rows = far_values
    gate_own, up_own, down_own = [
        sum(f + n, t(0)) for t, f, n in zip(wide_terms, first, second)
    ]
    small_a, small_b, small_c = scatter_three(
        (
            both(terms_a(first_rows, grad_b), terms_a(branch_rows, out_first)),
            both(terms_b(first_rows, grad_c), terms_b(branch_rows, out_second)),
            terms_c(first_rows, grad_x),
        ),
        "xyz",
        bf16,
    )

    def z_columns(value):
        ends = [0, HID, 2 * HID, 2 * HID + CHAN, 2 * HID + 2 * CHAN]
        ends += [2 * HID + 2 * CHAN + HALF, 2 * HID + 2 * CHAN + 2 * HALF]
        halves = []
        for t in range(2):
            halves.append(
                jnp.concatenate(
                    [value[..., ends[i + t] : ends[i + t + 1]] for i in (0, 2, 4)], axis=-1
                )
            )
        stacked = jnp.stack(halves, axis=1)
        return stacked.reshape((4,) + stacked.shape[2:])

    def stacked_terms(*values):
        return [lambda step, v=v, a=a: pick(v, a, step) for v, a in values]

    sum_a = jnp.concatenate([gate_own, small_a], axis=1).reshape(2, 4, ROWS, -1)
    sum_b = jnp.concatenate([up_own, small_b], axis=1).reshape(4, 2, ROWS, -1)
    sum_c = jnp.concatenate([down_own, small_c], axis=1).reshape(4, 4, ROWS, -1)
    sum_a = sum_a.transpose(1, 0, 2, 3)
    sum_b = z_columns(sum_b.transpose(1, 0, 2, 3))
    sum_a, sum_b, sum_c, small, input_grad_chip, hidden_state = tie(
        sum_a, sum_b, sum_c, small, input_grad_chip, hidden_state
    )
    down_out = {k: dot_transposed(half_c(hidden_state, k), down_pieces[k]) for k in order}
    out_same = down_out[0] + jnp.where(z_even, down_out[1], down_out[3])
    out_other = down_out[2] + jnp.where(z_even, down_out[3], down_out[1])
    halves = jnp.where(low_z, out_same, out_other), jnp.where(low_z, out_other, out_same)
    down_sum = jnp.concatenate(
        [half[:, 128 * i : 128 * (i + 1)] for i in range(4) for half in halves], axis=1
    )
    mixed_chip = (middle + core_sum(down_sum)).astype(bf16)
    sum_a, sum_b, sum_c = scatter_three(
        stacked_terms((sum_a, "y"), (sum_b, "z"), (sum_c, "x")), "yzx", bf16
    )
    sum_a, sum_b, sum_c, mixed_chip = tie(z_columns(sum_a), sum_b, sum_c, mixed_chip)
    sum_a, sum_b, sum_c = scatter_three(
        stacked_terms((sum_a, "z"), (sum_b, "x"), (sum_c, "y")), "zxy", bf16, staged=False
    )
    grad_chip = jnp.concatenate([sum_a, sum_b, sum_c], axis=1)
    grad_quarters = to_device(first_core, grad_chip)

    grad_quarters, mixed_chip, input_grad_chip = tie(grad_quarters, mixed_chip, input_grad_chip)

    def to_owner(value):
        got = lax.ppermute(value, ("c", "zl"), [(0, 1), (3, 2)])
        return jnp.where(own_sequence, value, got)

    mixed = to_owner(mixed_chip)
    input_grad = to_owner(input_grad_chip)

    updated = momentum_decay * momentum_chip + grad_chip
    total_columns = updated.shape[1]
    members = 32
    blocks = -(-total_columns // (members * BLK))
    share = blocks * BLK
    filled = jnp.pad(updated, ((0, 0), (0, share * members - total_columns)))
    slices = jnp.pad(small.reshape(members, -1), ((0, 0), (0, 2 * BLK - small.shape[0] // members)))
    slices = slices.reshape(members, 2, BLK).transpose(1, 0, 2)
    slices = jnp.pad(slices, ((0, ROWS - 2), (0, 0), (0, 0)))
    filled = jnp.concatenate([filled.reshape(ROWS, members, share), slices], axis=2)
    plane = ("x", "zh", "y")
    owned = lax.all_to_all(
        filled.reshape(ROWS, -1), plane, split_axis=1, concat_axis=0, tiled=True
    )
    slice_sum = jnp.sum(owned.reshape(members, ROWS, -1)[:, :2, share:], axis=0)
    finished = newton_schulz(owned[:, :share])
    terms = []
    for _ in range(3):
        term = lax.reduce_precision(slice_sum, 8, 7)
        terms.append(term)
        slice_sum = slice_sum - term
    terms = jnp.pad(jnp.concatenate(terms, axis=0), ((0, ROWS - 6), (0, 0)))
    terms = jnp.broadcast_to(terms[None], (members, ROWS, BLK)).reshape(D, BLK)
    finished = jnp.concatenate([finished, terms], axis=1).astype(bf16)
    returned = lax.all_to_all(finished, plane, split_axis=0, concat_axis=1, tiled=True)
    returned = returned.reshape(ROWS, members, share + BLK)
    ortho_chip = returned[:, :, :share].reshape(ROWS, -1)[:, :total_columns]
    terms = returned[:6, :, share:].astype(f32)
    summed = (terms[0:2] + terms[2:4] + terms[4:6]).transpose(1, 0, 2).reshape(members, -1)
    summed = summed[:, : small.shape[0] // members].reshape(-1)
    gains_grad = summed[: 2 * D].reshape(2, D)
    tap_sums = summed[2 * D :].reshape(KS, 2, CHAN)
    tap_mine = lax.dynamic_index_in_dim(tap_sums, z_low, 1, keepdims=False)
    tap_other = swap_cores(tap_mine)
    kernel_grad = jnp.where(
        first_core,
        jnp.concatenate([tap_mine, tap_other], axis=1),
        jnp.concatenate([tap_other, tap_mine], axis=1),
    )

    grads = unpack(*grad_quarters)
    ortho = unpack(*to_device(first_core, ortho_chip))
    momenta = (input_momentum, output_momentum, gate_momentum, up_momentum, down_momentum)
    params = (
        input_projection,
        output_projection,
        gate_projection,
        up_projection,
        down_projection,
    )
    momenta_new = [momentum_decay * m + g for m, g in zip(momenta, grads)]
    muon_rate = 0.25 * (D / BLK) ** 0.5
    params_new = [p - muon_rate * o.astype(f32) for p, o in zip(params, ortho)]
    gains_var_new, gains_new = adam_update(norm_gains, gains_mean, gains_var, gains_grad)
    kernel_var_new, kernel_new = adam_update(kernel, kernel_mean, kernel_var, kernel_grad)
    return (
        mixed,
        input_grad,
        *grads,
        *momenta_new,
        *params_new,
        gains_grad,
        gains_var_new,
        gains_new,
        kernel_grad,
        kernel_var_new,
        kernel_new,
    )


def solution(mesh):
    torus = Mesh(mesh.devices.reshape(4, 2, 4, 2, 2), AXES)
    dp, tensor = ("x", "zh", "y", "c"), "zl"
    token = P(dp, None)
    in_proj, wide, tall = P(dp, None, tensor), P(dp, tensor), P(tensor, dp)
    taps = P(None, tensor)
    matrices = (in_proj, tall, wide, wide, tall)
    in_specs = (token, token, P(), P(), P(), taps, taps, taps) + tuple(
        spec for spec in matrices for _ in range(2)
    )
    out_specs = (token, token) + matrices * 3 + (P(), P(), P(), taps, taps, taps)
    return jax.shard_map(
        per_device, mesh=torus, in_specs=in_specs, out_specs=out_specs, check_vma=False
    )
```
